512 devices in a mesh: gx: 64 (over y_hi, z, core), gy: 8 (over x, y_lo).
Axes of the slice: x: 4, y: 8 (y_hi: 4, y_lo: 2; y = y_hi * 2 + y_lo), z: 8, core: 2. Of those that a mesh axis runs over, the one named last changes fastest.
Arguments:
- e_field: float32 [3, 16, 1024, 1024], P(None, None, 'gx', 'gy'), may hold values from -6 to 6
- h_field: float32 [3, 16, 1024, 1024], P(None, None, 'gx', 'gy'), may hold values from -6 to 6
- pole_now: float32 [2, 3, 16, 1024, 1024], P(None, None, None, 'gx', 'gy'), may hold values from -6 to 6
- pole_prev: float32 [2, 3, 16, 1024, 1024], P(None, None, None, 'gx', 'gy'), may hold values from -6 to 6
- material: int32 [16, 1024, 1024], P(None, 'gx', 'gy'), may hold values from 0 to 3, as said below
- eps_inf: float32 [4], replicated, may hold values from 1.5 to 6
- resonance: float32 [4, 2], replicated, may hold values from 0.3 to 1.6
- damping: float32 [4, 2], replicated, may hold values from 0.05 to 1
- strength: float32 [4, 2], replicated, may hold values from 0.5 to 3
Outputs:
- e_out: float32 [3, 16, 1024, 1024], P(None, None, 'gx', 'gy')
- h_out: float32 [3, 16, 1024, 1024], P(None, None, 'gx', 'gy')
The draws below stay inside these ranges and needn't reach their ends.
Inputs may be any that keep to these rules, and one draw needn't show every extreme that they name: `material`: 0 perovskite, 1 ITO junction, 2 silicon, 3 air; along z each column runs air, perovskite, junction, silicon, each layer at least one cell thick, with interface depths varying from column to column.
All inputs are finite; a program needn't handle non-finite values.
Results may differ from the reference program's by a relative error of at most 0.0001.
Values sent between devices are 32-bit elements; how exact they have to be, the bound alone decides.
A program may use at most 128 MiB of HBM per device.

```python
import math
import jax
import jax.numpy as jnp

NZ = 16
MATERIALS = 4
POLES = 2
NX = 1024
NY = 1024


def draw_material(key, part):
    key = jax.random.fold_in(key, 11)
    first, second, third = jax.random.split(key, 3)
    top_depth = jax.random.randint(first, (NX, NY), 1, 4)
    perov_end = top_depth + jax.random.randint(second, (NX, NY), 3, 7)
    junction_end = perov_end + jax.random.randint(third, (NX, NY), 1, 3)
    layer = jnp.arange(NZ, dtype=jnp.int32)[:, None, None]
    return jnp.where(layer < top_depth[None], 3, jnp.where(layer < perov_end[None], 0, jnp.where(layer < junction_end[None], 1, 2))).astype(jnp.int32)


def steps_of(key, shape, cuts, least, high):
    def one(position, shards_of):
        draws = jax.random.uniform(jax.random.fold_in(jax.random.fold_in(key, 6), position), (shards_of,), jnp.float32, least / len(cuts), high / len(cuts))
        return jnp.repeat(jnp.exp(draws), shape[position] // shards_of).reshape((-1,) + (1,) * (len(shape) - position - 1))

    gain = one(*cuts[0])
    for cut in cuts[1:]:
        gain = gain * one(*cut)
    return gain


def bell_draw(stream_key, dims, width, reach, cuts=(), kind=jnp.bfloat16):
    values = jax.random.normal(stream_key, dims, jnp.float32) * width
    if len(cuts) > 0:
        values = steps_of(stream_key, dims, cuts, -0.22, 0.18) * values
    return jnp.clip(values, min=-reach, max=reach).astype(kind)


def setup_inputs(seed: int = 0) -> dict:
    seeds = jax.random.split(jax.random.key(seed), 10)
    e_field = bell_draw(seeds[0], (3, NZ, NX, NY), 1.0, 6.0, ((2, 64), (3, 8)), jnp.float32)
    h_field = bell_draw(seeds[1], (3, NZ, NX, NY), 1.0, 6.0, ((2, 64), (3, 8)), jnp.float32)
    pole_now = bell_draw(seeds[2], (POLES, 3, NZ, NX, NY), 0.5, 6.0, ((3, 64), (4, 8)), jnp.float32)
    pole_prev = bell_draw(seeds[3], (POLES, 3, NZ, NX, NY), 0.5, 6.0, ((3, 64), (4, 8)), jnp.float32)
    material = draw_material(jax.random.fold_in(seeds[9], 71), 0)
    eps_inf = jnp.clip(jnp.exp(jax.random.uniform(seeds[5], (MATERIALS,), jnp.float32, math.log(1.5), math.log(6.0))), 1.5, 6.0)
    resonance = jnp.clip(jnp.exp(jax.random.uniform(seeds[6], (MATERIALS, POLES), jnp.float32, math.log(0.3), math.log(1.6))), 0.3, 1.6)
    damping = jnp.clip(jnp.exp(jax.random.uniform(seeds[7], (MATERIALS, POLES), jnp.float32, math.log(0.05), math.log(1.0))), 0.05, 1.0)
    strength = jnp.clip(jnp.exp(jax.random.uniform(seeds[8], (MATERIALS, POLES), jnp.float32, math.log(0.5), math.log(3.0))), 0.5, 3.0)
    return dict(e_field=e_field, h_field=h_field, pole_now=pole_now, pole_prev=pole_prev, material=material, eps_inf=eps_inf, resonance=resonance, damping=damping, strength=strength)


time_step = 0.5


def cell_values(material, table):
    total = jnp.zeros(table.shape[1:] + material.shape, jnp.float32)
    for index in range(table.shape[0]):
        entry = table[index].reshape(table.shape[1:] + (1,) * material.ndim)
        total = total + jnp.where(material[None] == index, entry, jnp.float32(0.0))
    return total


def coefficients(material, eps_inf, resonance, damping, strength):
    air = jnp.arange(eps_inf.shape[0]) == 3
    eps_tab = jnp.where(air, jnp.float32(1.0), eps_inf)
    str_tab = jnp.where(air[:, None], jnp.float32(0.0), strength)
    wdt = resonance * resonance * (time_step * time_step)
    denom = 1.0 + damping * (time_step / 2.0)
    one_tab = (2.0 - wdt) / denom
    two_tab = (damping * (time_step / 2.0) - 1.0) / denom
    three_tab = str_tab * wdt / denom
    inv_eps = 1.0 / cell_values(material, eps_tab[:, None])[0]
    return cell_values(material, one_tab), cell_values(material, two_tab), cell_values(material, three_tab), inv_eps


def forward_z(field):
    return jnp.concatenate([field[1:], jnp.zeros_like(field[:1])], 0) - field


def backward_z(field):
    return field - jnp.concatenate([jnp.zeros_like(field[:1]), field[:-1]], 0)


def reference(e_field, h_field, pole_now, pole_prev, material, eps_inf, resonance, damping, strength):
    coef_one, coef_two, coef_three, inv_eps = coefficients(material, eps_inf, resonance, damping, strength)
    for step in range(2):
        ex, ey, ez = e_field[0], e_field[1], e_field[2]
        hx, hy, hz = h_field[0], h_field[1], h_field[2]
        dx_ey = jnp.roll(ey, -1, 1) - ey
        dx_ez = jnp.roll(ez, -1, 1) - ez
        dy_ex = jnp.roll(ex, -1, 2) - ex
        dy_ez = jnp.roll(ez, -1, 2) - ez
        hx = hx - time_step * (dy_ez - forward_z(ey))
        hy = hy - time_step * (forward_z(ex) - dx_ez)
        hz = hz - time_step * (dx_ey - dy_ex)
        fresh = coef_one[:, None] * pole_now + coef_two[:, None] * pole_prev + coef_three[:, None] * e_field[None]
        bx_hy = hy - jnp.roll(hy, 1, 1)
        bx_hz = hz - jnp.roll(hz, 1, 1)
        by_hx = hx - jnp.roll(hx, 1, 2)
        by_hz = hz - jnp.roll(hz, 1, 2)
        curl = jnp.stack([by_hz - backward_z(hy), backward_z(hx) - bx_hz, bx_hy - by_hx])
        change = jnp.sum(fresh - pole_now, axis=0)
        e_field = e_field + (time_step * curl - change) * inv_eps[None]
        h_field = jnp.stack([hx, hy, hz])
        pole_prev = pole_now
        pole_now = fresh
    return e_field, h_field
```

```python
import jax
import jax.numpy as jnp
from jax import lax
from jax.experimental import pallas as pl
from jax.experimental.pallas import tpu as pltpu
from jax.sharding import PartitionSpec as P

MESH = pl.DeviceIdType.MESH
DT = 0.5
NZ = 16
ROWS = 16
LANES = 128
TOP = 8
END = TOP + ROWS
TILE = (8, LANES)


def fill_tables(tables, eps_ref, res_ref, damp_ref, str_ref):
    for m in range(4):
        one = jnp.ones(TILE, jnp.float32)
        inv = one if m == 3 else one / jnp.full(TILE, eps_ref[m])
        c3_sum = jnp.zeros(TILE, jnp.float32)
        r = jnp.zeros(TILE, jnp.float32)
        for k in range(2):
            res = jnp.full(TILE, res_ref[m, k])
            damp = jnp.full(TILE, damp_ref[m, k])
            gain = jnp.full(TILE, str_ref[m, k])
            if m == 3:
                gain = jnp.zeros(TILE, jnp.float32)
            w = res * res * (DT * DT)
            s = 1.0 + damp * (DT / 2.0)
            c1 = (2.0 - w) / s
            c2 = (damp * (DT / 2.0) - 1.0) / s
            c3 = gain * w / s
            g = inv * (1.0 - c1)
            h = -inv * c2
            tables[2 + k, m] = g
            tables[4 + k, m] = h
            tables[6 + k, m] = g * c1 + h
            tables[8 + k, m] = g * c2
            c3_sum = c3_sum + c3
            r = r + g * c3
        tables[0, m] = 1.0 - inv * c3_sum
        tables[1, m] = inv * DT
        tables[10, m] = r


def kernel(
    e_hbm, h_hbm, now_hbm, prev_hbm, mat_hbm, eps_ref, res_ref, damp_ref, str_ref,
    e_out, h_out,
    eh, ad, now, prev, mat, tables, keep, late, h1, e1, h2, e2, strips, wide, sh1, se1, sh2,
    load_sem, send_sem, recv_sem, out_sem,
):
    gx, gy = lax.axis_index("gx"), lax.axis_index("gy")
    nx, ny = lax.axis_size("gx"), lax.axis_size("gy")
    xp, xn = lax.rem(gx + nx - 1, nx), lax.rem(gx + 1, nx)
    yp, yn = lax.rem(gy + ny - 1, ny), lax.rem(gy + 1, ny)

    loads = [
        pltpu.make_async_copy(e_hbm, eh.at[0:3, 1 : NZ + 1, TOP:END, :], load_sem.at[0]),
        pltpu.make_async_copy(h_hbm, eh.at[3:6, 1 : NZ + 1, TOP:END, :], load_sem.at[1]),
        pltpu.make_async_copy(mat_hbm, mat, load_sem.at[2]),
        pltpu.make_async_copy(now_hbm, now, load_sem.at[3]),
        pltpu.make_async_copy(prev_hbm, prev, load_sem.at[4]),
    ]
    barrier = pltpu.get_barrier_semaphore()
    for d in ((xp, gy), (xn, gy), (gx, yp), (gx, yn), (xp, yp), (xp, yn), (xn, yp), (xn, yn)):
        pl.semaphore_signal(barrier, inc=1, device_id=d, device_id_type=MESH)
    for c in loads:
        c.start()
    fill_tables(tables, eps_ref, res_ref, damp_ref, str_ref)
    zero = jnp.zeros((40, LANES), jnp.float32)
    for c in range(3):
        eh[c, NZ + 1] = zero
        e1[c, NZ] = zero
        h1[c, 0] = zero
        h2[c, 0] = zero
    pl.semaphore_wait(barrier, 8)

    def send(index, src, dst, device):
        c = pltpu.make_async_remote_copy(
            src_ref=src, dst_ref=dst, send_sem=send_sem.at[index], recv_sem=recv_sem.at[index],
            device_id=device, device_id_type=MESH,
        )
        c.start()
        return c

    inside = pl.ds(1, NZ)
    sends = [
        send(0, e_hbm.at[:, :, 14:16, :], eh.at[0:3, inside, 6:8, :], (xn, gy)),
        send(1, h_hbm.at[:, :, 14:16, :], eh.at[3:6, inside, 6:8, :], (xn, gy)),
        send(2, e_hbm.at[:, :, 0:2, :], eh.at[0:3, inside, 24:26, :], (xp, gy)),
        send(3, h_hbm.at[:, :, 0:1, :], eh.at[3:6, inside, 24:25, :], (xp, gy)),
    ]
    for c in loads:
        c.wait()

    def local(z, _):
        for b in (0, 8):
            kind = mat[z, b : b + 8, :]
            low = (kind & 1) == 1
            high = kind >= 2

            def value(i):
                return jnp.where(
                    high,
                    jnp.where(low, tables[i, 3], tables[i, 2]),
                    jnp.where(low, tables[i, 1], tables[i, 0]),
                )

            e, d, g0, g1, w0, w1, p0, p1, q0, q1, r = [value(i) for i in range(11)]
            rows = slice(TOP + b, TOP + b + 8)
            keep[z, b : b + 8, :] = e
            ad[3, z, rows, :] = d
            for c in range(3):
                f = eh[c, z + 1, rows, :]
                n0, n1 = now[0, c, z, b : b + 8, :], now[1, c, z, b : b + 8, :]
                m0, m1 = prev[0, c, z, b : b + 8, :], prev[1, c, z, b : b + 8, :]
                ad[c, z, rows, :] = (e * f + (g0 * n0 + g1 * n1)) + (w0 * m0 + w1 * m1)
                late[c, z, b : b + 8, :] = (r * f + (p0 * n0 + p1 * n1)) + (q0 * m0 + q1 * m1)
        return 0

    lax.fori_loop(0, NZ, local, 0)

    lane = lax.broadcasted_iota(jnp.int32, TILE, 1)
    group = lane // 8
    slot = lane % 8

    def pack(z, held):
        mine = group == z
        out = []
        for i in range(10):
            for b in (0, 8):
                rows = slice(TOP + b, TOP + b + 8)
                f = eh[i, z + 1, rows, :] if i < 6 else ad[i - 6, z, rows, :]
                out.append(jnp.where(mine, pltpu.roll(f, 8 * z + 2, 1), held[len(out)]))
        return tuple(out)

    held = lax.fori_loop(0, NZ, pack, tuple(jnp.zeros(TILE, jnp.float32) for _ in range(20)))
    for i in range(10):
        for j in range(2):
            strips[0, i, TOP + 8 * j : TOP + 8 * j + 8, :] = held[2 * i + j]

    own = strips.at[0]
    sends += [
        send(4, own.at[:, TOP:END, :], strips.at[1, :, TOP:END, :], (gx, yn)),
        send(5, own.at[:, TOP:END, :], strips.at[2, :, TOP:END, :], (gx, yp)),
        send(6, ad.at[:, :, 23:24, :], ad.at[:, :, 7:8, :], (xn, gy)),
        send(7, ad.at[:, :, 8:9, :], ad.at[:, :, 24:25, :], (xp, gy)),
        send(8, own.at[:, 22:24, :], strips.at[0, :, 6:8, :], (xn, gy)),
        send(9, own.at[:, 8:10, :], strips.at[0, :, 24:26, :], (xp, gy)),
        send(10, own.at[:, 22:24, :], strips.at[1, :, 6:8, :], (xn, yn)),
        send(11, own.at[:, 22:24, :], strips.at[2, :, 6:8, :], (xn, yp)),
        send(12, own.at[:, 8:10, :], strips.at[1, :, 24:26, :], (xp, yn)),
        send(13, own.at[:, 8:10, :], strips.at[2, :, 24:26, :], (xp, yp)),
    ]
    for c in sends:
        c.wait_recv()

    for i in range(10):
        for r in (6, 14, 22):
            rows = slice(r, r + 8)
            me, before, after = strips[0, i, rows, :], strips[1, i, rows, :], strips[2, i, rows, :]
            wide[i, rows, :] = jnp.where(
                slot < 4,
                jnp.where(slot < 2, me, after),
                pltpu.roll(jnp.where(slot < 2, before, me), 4, 1),
            )

    def ahead_z(f):
        return jnp.where(lane < 120, pltpu.roll(f, 120, 1), 0.0)

    def behind_z(f):
        return jnp.where(lane >= 8, pltpu.roll(f, 8, 1), 0.0)

    def h_step(ex, ey, ez, hx, hy, hz, ex_y, ez_y, ey_x, ez_x, ex_z, ey_z):
        return (
            hx - DT * ((ez_y - ez) - (ey_z - ey)),
            hy - DT * ((ex_z - ex) - (ez_x - ez)),
            hz - DT * ((ey_x - ey) - (ex_y - ex)),
        )

    def curl(hx, hy, hz, hx_y, hz_y, hy_x, hz_x, hx_z, hy_z):
        return (
            (hz - hz_y) - (hy - hy_z),
            (hx - hx_z) - (hz - hz_x),
            (hy - hy_x) - (hx - hx_y),
        )

    def strip_h(e_ref, h_ref, base, out, starts):
        for r in starts:
            rows, next_rows = slice(r, r + 8), slice(r + 1, r + 9)
            ex, ey, ez = (e_ref[i, rows, :] for i in range(3))
            new = h_step(
                ex, ey, ez, *(h_ref[base + i, rows, :] for i in range(3)),
                pltpu.roll(ex, 127, 1), pltpu.roll(ez, 127, 1),
                e_ref[1, next_rows, :], e_ref[2, next_rows, :], ahead_z(ex), ahead_z(ey),
            )
            for i in range(3):
                out[i, rows, :] = new[i]

    strip_h(wide, wide, 3, sh1, (6, 14, 22))
    for r in (7, 15, 23):
        rows, back_rows = slice(r, r + 8), slice(r - 1, r + 7)
        hx, hy, hz = (sh1[i, rows, :] for i in range(3))
        turn = curl(
            hx, hy, hz, pltpu.roll(hx, 1, 1), pltpu.roll(hz, 1, 1),
            sh1[1, back_rows, :], sh1[2, back_rows, :], behind_z(hx), behind_z(hy),
        )
        d = wide[9, rows, :]
        for i in range(3):
            se1[i, rows, :] = wide[6 + i, rows, :] + d * turn[i]
    strip_h(se1, sh1, 0, sh2, (7, 15, 23))

    def main_h(e_ref, shift, h_ref, h_base, strip, out, starts):
        def body(z, _):
            far = 125 - 8 * z
            for r in starts:
                rows, next_rows = slice(r, r + 8), slice(r + 1, r + 9)
                ex, ey, ez = (e_ref[i, z + shift, rows, :] for i in range(3))
                new = h_step(
                    ex, ey, ez, *(h_ref[h_base + i, z + 1, rows, :] for i in range(3)),
                    jnp.where(lane == 127, pltpu.roll(strip[0, rows, :], far, 1), pltpu.roll(ex, 127, 1)),
                    jnp.where(lane == 127, pltpu.roll(strip[2, rows, :], far, 1), pltpu.roll(ez, 127, 1)),
                    e_ref[1, z + shift, next_rows, :], e_ref[2, z + shift, next_rows, :],
                    e_ref[0, z + shift + 1, rows, :], e_ref[1, z + shift + 1, rows, :],
                )
                for i in range(3):
                    out[i, z + 1, rows, :] = new[i]
            return 0

        lax.fori_loop(0, NZ, body, 0, unroll=2)

    def main_curl(h_ref, z, r, strip):
        rows, back_rows = slice(r, r + 8), slice(r - 1, r + 7)
        far = 123 - 8 * z
        hx, hy, hz = (h_ref[i, z + 1, rows, :] for i in range(3))
        return curl(
            hx, hy, hz,
            jnp.where(lane == 0, pltpu.roll(strip[0, rows, :], far, 1), pltpu.roll(hx, 1, 1)),
            jnp.where(lane == 0, pltpu.roll(strip[2, rows, :], far, 1), pltpu.roll(hz, 1, 1)),
            h_ref[1, z + 1, back_rows, :], h_ref[2, z + 1, back_rows, :],
            h_ref[0, z, rows, :], h_ref[1, z, rows, :],
        )

    main_h(eh, 1, eh, 3, wide, h1, (6, 14, 22))

    def first_e(z, _):
        for r in (7, 15, 23):
            rows = slice(r, r + 8)
            turn = main_curl(h1, z, r, sh1)
            d = ad[3, z, rows, :]
            for i in range(3):
                e1[i, z, rows, :] = ad[i, z, rows, :] + d * turn[i]
        return 0

    lax.fori_loop(0, NZ, first_e, 0, unroll=2)
    main_h(e1, 0, h1, 0, se1, h2, (7, 15, 23))
    h_write = pltpu.make_async_copy(h2.at[:, inside, TOP:END, :], h_out, out_sem.at[0])
    h_write.start()

    def second_e(z, _):
        for b in (0, 8):
            rows, here = slice(TOP + b, TOP + b + 8), slice(b, b + 8)
            turn = main_curl(h2, z, TOP + b, sh2)
            d, factor = ad[3, z, rows, :], keep[z, here, :]
            for i in range(3):
                e2[i, z, here, :] = factor * e1[i, z, rows, :] + d * turn[i] + late[i, z, here, :]
        return 0

    lax.fori_loop(0, NZ, second_e, 0, unroll=2)
    e_write = pltpu.make_async_copy(e2, e_out, out_sem.at[1])
    e_write.start()
    for c in sends:
        c.wait_send()
    h_write.wait()
    e_write.wait()


def body(e_field, h_field, pole_now, pole_prev, material, eps_inf, resonance, damping, strength):
    anywhere = pl.BlockSpec(memory_space=pl.ANY)
    scalars = pl.BlockSpec(memory_space=pltpu.SMEM)
    f32 = jnp.float32
    block = jax.ShapeDtypeStruct(e_field.shape, f32)
    return pl.pallas_call(
        kernel,
        out_shape=(block, block),
        in_specs=[anywhere] * 5 + [scalars] * 4,
        out_specs=(anywhere, anywhere),
        scratch_shapes=[
            pltpu.VMEM((6, NZ + 2, 40, LANES), f32),
            pltpu.VMEM((4, NZ, 40, LANES), f32),
            pltpu.VMEM(pole_now.shape, f32),
            pltpu.VMEM(pole_prev.shape, f32),
            pltpu.VMEM(material.shape, jnp.int32),
            pltpu.VMEM((11, 4) + TILE, f32),
            pltpu.VMEM((NZ, ROWS, LANES), f32),
            pltpu.VMEM((3, NZ, ROWS, LANES), f32),
            pltpu.VMEM((3, NZ + 1, 40, LANES), f32),
            pltpu.VMEM((3, NZ + 1, 40, LANES), f32),
            pltpu.VMEM((3, NZ + 1, 40, LANES), f32),
            pltpu.VMEM((3, NZ, ROWS, LANES), f32),
            pltpu.VMEM((3, 10, 40, LANES), f32),
            pltpu.VMEM((10, 40, LANES), f32),
            pltpu.VMEM((3, 40, LANES), f32),
            pltpu.VMEM((3, 40, LANES), f32),
            pltpu.VMEM((3, 40, LANES), f32),
            pltpu.SemaphoreType.DMA((5,)),
            pltpu.SemaphoreType.DMA((14,)),
            pltpu.SemaphoreType.DMA((14,)),
            pltpu.SemaphoreType.DMA((2,)),
        ],
        compiler_params=pltpu.CompilerParams(
            collective_id=0, has_side_effects=True, vmem_limit_bytes=48 * 1024 * 1024
        ),
    )(e_field, h_field, pole_now, pole_prev, material, eps_inf, resonance, damping, strength)


def solution(mesh):
    field = P(None, None, "gx", "gy")
    pole = P(None, None, None, "gx", "gy")
    in_specs = (field, field, pole, pole, P(None, "gx", "gy"), P(), P(), P(), P())
    return jax.shard_map(
        body, mesh=mesh, in_specs=in_specs, out_specs=(field, field), check_vma=False
    )
```

```python
import jax
import jax.numpy as jnp
from jax import lax
from jax.experimental import pallas as pl
from jax.experimental.pallas import tpu as pltpu
from jax.sharding import PartitionSpec as P

MESH = pl.DeviceIdType.MESH
DT = 0.5
NZ = 16
ROWS = 16
LANES = 128
TOP = 8
END = TOP + ROWS
TILE = (8, LANES)


def fill_tables(tables, eps_ref, res_ref, damp_ref, str_ref):
    for m in range(4):
        one = jnp.ones(TILE, jnp.float32)
        inv = one if m == 3 else one / jnp.full(TILE, eps_ref[m])
        c3_sum = jnp.zeros(TILE, jnp.float32)
        r = jnp.zeros(TILE, jnp.float32)
        for k in range(2):
            res = jnp.full(TILE, res_ref[k, m])
            damp = jnp.full(TILE, damp_ref[k, m])
            gain = jnp.full(TILE, str_ref[k, m])
            if m == 3:
                gain = jnp.zeros(TILE, jnp.float32)
            w = res * res * (DT * DT)
            s = 1.0 + damp * (DT / 2.0)
            c1 = (2.0 - w) / s
            c2 = (damp * (DT / 2.0) - 1.0) / s
            c3 = gain * w / s
            g = inv * (1.0 - c1)
            h = -inv * c2
            tables[2 + k, m] = g
            tables[4 + k, m] = h
            tables[6 + k, m] = g * c1 + h
            tables[8 + k, m] = g * c2
            c3_sum = c3_sum + c3
            r = r + g * c3
        tables[0, m] = 1.0 - inv * c3_sum
        tables[1, m] = inv * DT
        tables[10, m] = r


def kernel(
    e_hbm, h_hbm, now_hbm, prev_hbm, mat_hbm, eps_hbm, res_hbm, damp_hbm, str_hbm,
    e_out, h_out,
    eps_ref, res_ref, damp_ref, str_ref,
    eh, ad, now, prev, mat, tables, keep, late, h1, e1, h2, strips, wide, sh1, se1, sh2,
    load_sem, send_sem, recv_sem,
):
    gx, gy = lax.axis_index("gx"), lax.axis_index("gy")
    nx, ny = lax.axis_size("gx"), lax.axis_size("gy")
    xp, xn = lax.rem(gx + nx - 1, nx), lax.rem(gx + 1, nx)
    yp, yn = lax.rem(gy + ny - 1, ny), lax.rem(gy + 1, ny)

    loads = [
        pltpu.make_async_copy(e_hbm, eh.at[0:3, 1 : NZ + 1, TOP:END, :], load_sem.at[0]),
        pltpu.make_async_copy(h_hbm, eh.at[3:6, 1 : NZ + 1, TOP:END, :], load_sem.at[1]),
        pltpu.make_async_copy(mat_hbm, mat, load_sem.at[2]),
        pltpu.make_async_copy(now_hbm, now, load_sem.at[3]),
        pltpu.make_async_copy(prev_hbm, prev, load_sem.at[4]),
    ]
    barrier = pltpu.get_barrier_semaphore()
    for d in ((xp, gy), (xn, gy), (gx, yp), (gx, yn), (xp, yp), (xp, yn), (xn, yp), (xn, yn)):
        pl.semaphore_signal(barrier, inc=1, device_id=d, device_id_type=MESH)
    small = [
        pltpu.make_async_copy(src, dst, load_sem.at[5 + i])
        for i, (src, dst) in enumerate(
            ((eps_hbm, eps_ref), (res_hbm, res_ref), (damp_hbm, damp_ref), (str_hbm, str_ref))
        )
    ]
    for c in small + loads:
        c.start()
    for c in small:
        c.wait()
    fill_tables(tables, eps_ref, res_ref, damp_ref, str_ref)
    zero = jnp.zeros((40, LANES), jnp.float32)
    for c in range(3):
        eh[c, NZ + 1] = zero
        e1[c, NZ] = zero
        h1[c, 0] = zero
        h2[c, 0] = zero
    pl.semaphore_wait(barrier, 8)

    def send(index, src, dst, device):
        c = pltpu.make_async_remote_copy(
            src_ref=src, dst_ref=dst, send_sem=send_sem.at[index], recv_sem=recv_sem.at[index],
            device_id=device, device_id_type=MESH,
        )
        c.start()
        return c

    inside = pl.ds(1, NZ)
    sends = [
        send(0, e_hbm.at[:, :, 14:16, :], eh.at[0:3, inside, 6:8, :], (xn, gy)),
        send(1, h_hbm.at[:, :, 14:16, :], eh.at[3:6, inside, 6:8, :], (xn, gy)),
        send(2, e_hbm.at[:, :, 0:2, :], eh.at[0:3, inside, 24:26, :], (xp, gy)),
        send(3, h_hbm.at[:, :, 0:1, :], eh.at[3:6, inside, 24:25, :], (xp, gy)),
    ]
    for c in loads:
        c.wait()

    def local(z, _):
        for b in (0, 8):
            kind = mat[z, b : b + 8, :]
            low = (kind & 1) == 1
            high = kind >= 2

            def value(i):
                return jnp.where(
                    high,
                    jnp.where(low, tables[i, 3], tables[i, 2]),
                    jnp.where(low, tables[i, 1], tables[i, 0]),
                )

            e, d, g0, g1, w0, w1, p0, p1, q0, q1, r = [value(i) for i in range(11)]
            rows = slice(TOP + b, TOP + b + 8)
            keep[z, b : b + 8, :] = e
            ad[3, z, rows, :] = d
            for c in range(3):
                f = eh[c, z + 1, rows, :]
                n0, n1 = now[0, c, z, b : b + 8, :], now[1, c, z, b : b + 8, :]
                m0, m1 = prev[0, c, z, b : b + 8, :], prev[1, c, z, b : b + 8, :]
                ad[c, z, rows, :] = (e * f + (g0 * n0 + g1 * n1)) + (w0 * m0 + w1 * m1)
                late[c, z, b : b + 8, :] = (r * f + (p0 * n0 + p1 * n1)) + (q0 * m0 + q1 * m1)
        return 0

    lax.fori_loop(0, NZ, local, 0)

    lane = lax.broadcasted_iota(jnp.int32, TILE, 1)
    group = lane // 8
    slot = lane % 8

    def pack(z, held):
        mine = group == z
        out = []
        for i in range(10):
            for b in (0, 8):
                rows = slice(TOP + b, TOP + b + 8)
                f = eh[i, z + 1, rows, :] if i < 6 else ad[i - 6, z, rows, :]
                out.append(jnp.where(mine, pltpu.roll(f, 8 * z + 2, 1), held[len(out)]))
        return tuple(out)

    held = lax.fori_loop(0, NZ, pack, tuple(jnp.zeros(TILE, jnp.float32) for _ in range(20)))
    for i in range(10):
        for j in range(2):
            strips[0, i, TOP + 8 * j : TOP + 8 * j + 8, :] = held[2 * i + j]

    own = strips.at[0]
    sends += [
        send(4, own.at[:, TOP:END, :], strips.at[1, :, TOP:END, :], (gx, yn)),
        send(5, own.at[:, TOP:END, :], strips.at[2, :, TOP:END, :], (gx, yp)),
        send(6, ad.at[:, :, 23:24, :], ad.at[:, :, 7:8, :], (xn, gy)),
        send(7, ad.at[:, :, 8:9, :], ad.at[:, :, 24:25, :], (xp, gy)),
        send(8, own.at[:, 22:24, :], strips.at[0, :, 6:8, :], (xn, gy)),
        send(9, own.at[:, 8:10, :], strips.at[0, :, 24:26, :], (xp, gy)),
        send(10, own.at[:, 22:24, :], strips.at[1, :, 6:8, :], (xn, yn)),
        send(11, own.at[:, 22:24, :], strips.at[2, :, 6:8, :], (xn, yp)),
        send(12, own.at[:, 8:10, :], strips.at[1, :, 24:26, :], (xp, yn)),
        send(13, own.at[:, 8:10, :], strips.at[2, :, 24:26, :], (xp, yp)),
    ]
    for c in sends:
        c.wait_recv()

    for i in range(10):
        for r in (6, 14, 22):
            rows = slice(r, r + 8)
            me, before, after = strips[0, i, rows, :], strips[1, i, rows, :], strips[2, i, rows, :]
            wide[i, rows, :] = jnp.where(
                slot < 4,
                jnp.where(slot < 2, me, after),
                pltpu.roll(jnp.where(slot < 2, before, me), 4, 1),
            )

    def ahead_z(f):
        return jnp.where(lane < 120, pltpu.roll(f, 120, 1), 0.0)

    def behind_z(f):
        return jnp.where(lane >= 8, pltpu.roll(f, 8, 1), 0.0)

    def h_step(ex, ey, ez, hx, hy, hz, ex_y, ez_y, ey_x, ez_x, ex_z, ey_z):
        return (
            hx - DT * ((ez_y - ez) - (ey_z - ey)),
            hy - DT * ((ex_z - ex) - (ez_x - ez)),
            hz - DT * ((ey_x - ey) - (ex_y - ex)),
        )

    def curl(hx, hy, hz, hx_y, hz_y, hy_x, hz_x, hx_z, hy_z):
        return (
            (hz - hz_y) - (hy - hy_z),
            (hx - hx_z) - (hz - hz_x),
            (hy - hy_x) - (hx - hx_y),
        )

    def strip_h(e_ref, h_ref, base, out, starts):
        for r in starts:
            rows, next_rows = slice(r, r + 8), slice(r + 1, r + 9)
            ex, ey, ez = (e_ref[i, rows, :] for i in range(3))
            new = h_step(
                ex, ey, ez, *(h_ref[base + i, rows, :] for i in range(3)),
                pltpu.roll(ex, 127, 1), pltpu.roll(ez, 127, 1),
                e_ref[1, next_rows, :], e_ref[2, next_rows, :], ahead_z(ex), ahead_z(ey),
            )
            for i in range(3):
                out[i, rows, :] = new[i]

    strip_h(wide, wide, 3, sh1, (6, 14, 22))
    for r in (7, 15, 23):
        rows, back_rows = slice(r, r + 8), slice(r - 1, r + 7)
        hx, hy, hz = (sh1[i, rows, :] for i in range(3))
        turn = curl(
            hx, hy, hz, pltpu.roll(hx, 1, 1), pltpu.roll(hz, 1, 1),
            sh1[1, back_rows, :], sh1[2, back_rows, :], behind_z(hx), behind_z(hy),
        )
        d = wide[9, rows, :]
        for i in range(3):
            se1[i, rows, :] = wide[6 + i, rows, :] + d * turn[i]
    strip_h(se1, sh1, 0, sh2, (7, 15, 23))

    def main_h(e_ref, shift, h_ref, h_base, strip, out, starts):
        def body(z, _):
            far = 125 - 8 * z
            for r in starts:
                rows, next_rows = slice(r, r + 8), slice(r + 1, r + 9)
                ex, ey, ez = (e_ref[i, z + shift, rows, :] for i in range(3))
                new = h_step(
                    ex, ey, ez, *(h_ref[h_base + i, z + 1, rows, :] for i in range(3)),
                    jnp.where(lane == 127, pltpu.roll(strip[0, rows, :], far, 1), pltpu.roll(ex, 127, 1)),
                    jnp.where(lane == 127, pltpu.roll(strip[2, rows, :], far, 1), pltpu.roll(ez, 127, 1)),
                    e_ref[1, z + shift, next_rows, :], e_ref[2, z + shift, next_rows, :],
                    e_ref[0, z + shift + 1, rows, :], e_ref[1, z + shift + 1, rows, :],
                )
                for i in range(3):
                    out[i, z + 1, rows, :] = new[i]
            return 0

        lax.fori_loop(0, NZ, body, 0, unroll=2)

    def main_curl(h_ref, z, r, strip):
        rows, back_rows = slice(r, r + 8), slice(r - 1, r + 7)
        far = 123 - 8 * z
        hx, hy, hz = (h_ref[i, z + 1, rows, :] for i in range(3))
        return curl(
            hx, hy, hz,
            jnp.where(lane == 0, pltpu.roll(strip[0, rows, :], far, 1), pltpu.roll(hx, 1, 1)),
            jnp.where(lane == 0, pltpu.roll(strip[2, rows, :], far, 1), pltpu.roll(hz, 1, 1)),
            h_ref[1, z + 1, back_rows, :], h_ref[2, z + 1, back_rows, :],
            h_ref[0, z, rows, :], h_ref[1, z, rows, :],
        )

    main_h(eh, 1, eh, 3, wide, h1, (6, 14, 22))

    def first_e(z, _):
        for r in (7, 15, 23):
            rows = slice(r, r + 8)
            turn = main_curl(h1, z, r, sh1)
            d = ad[3, z, rows, :]
            for i in range(3):
                e1[i, z, rows, :] = ad[i, z, rows, :] + d * turn[i]
        return 0

    lax.fori_loop(0, NZ, first_e, 0, unroll=2)
    main_h(e1, 0, h1, 0, se1, h2, (7, 15, 23))
    def second_e(z, _):
        for b in (0, 8):
            rows, here = slice(TOP + b, TOP + b + 8), slice(b, b + 8)
            turn = main_curl(h2, z, TOP + b, sh2)
            d, factor = ad[3, z, rows, :], keep[z, here, :]
            for i in range(3):
                h_out[i, z, here, :] = h2[i, z + 1, rows, :]
                e_out[i, z, here, :] = factor * e1[i, z, rows, :] + d * turn[i] + late[i, z, here, :]
        return 0

    lax.fori_loop(0, NZ, second_e, 0, unroll=2)
    for c in sends:
        c.wait_send()


def body(e_field, h_field, pole_now, pole_prev, material, eps_inf, resonance, damping, strength):
    hbm = pl.BlockSpec(memory_space=pltpu.HBM)
    vmem = pl.BlockSpec(memory_space=pltpu.VMEM)
    f32 = jnp.float32
    block = pltpu.VMEM(e_field.shape, f32)
    operands = (
        e_field, h_field, pole_now, pole_prev, material,
        eps_inf, resonance.T, damping.T, strength.T,
    )
    operands = [pltpu.with_memory_space_constraint(x, pltpu.HBM) for x in operands]
    return pl.pallas_call(
        kernel,
        out_shape=(block, block),
        in_specs=[hbm] * 9,
        out_specs=(vmem, vmem),
        scratch_shapes=[
            pltpu.SMEM((4,), f32),
            pltpu.SMEM((2, 4), f32),
            pltpu.SMEM((2, 4), f32),
            pltpu.SMEM((2, 4), f32),
            pltpu.VMEM((6, NZ + 2, 40, LANES), f32),
            pltpu.VMEM((4, NZ, 40, LANES), f32),
            pltpu.VMEM(pole_now.shape, f32),
            pltpu.VMEM(pole_prev.shape, f32),
            pltpu.VMEM(material.shape, jnp.int32),
            pltpu.VMEM((11, 4) + TILE, f32),
            pltpu.VMEM((NZ, ROWS, LANES), f32),
            pltpu.VMEM((3, NZ, ROWS, LANES), f32),
            pltpu.VMEM((3, NZ + 1, 40, LANES), f32),
            pltpu.VMEM((3, NZ + 1, 40, LANES), f32),
            pltpu.VMEM((3, NZ + 1, 40, LANES), f32),
            pltpu.VMEM((3, 10, 40, LANES), f32),
            pltpu.VMEM((10, 40, LANES), f32),
            pltpu.VMEM((3, 40, LANES), f32),
            pltpu.VMEM((3, 40, LANES), f32),
            pltpu.VMEM((3, 40, LANES), f32),
            pltpu.SemaphoreType.DMA((9,)),
            pltpu.SemaphoreType.DMA((14,)),
            pltpu.SemaphoreType.DMA((14,)),
        ],
        compiler_params=pltpu.CompilerParams(
            collective_id=0, has_side_effects=True, vmem_limit_bytes=48 * 1024 * 1024
        ),
    )(*operands)


def solution(mesh):
    field = P(None, None, "gx", "gy")
    pole = P(None, None, None, "gx", "gy")
    in_specs = (field, field, pole, pole, P(None, "gx", "gy"), P(), P(), P(), P())
    return jax.shard_map(
        body, mesh=mesh, in_specs=in_specs, out_specs=(field, field), check_vma=False
    )
```

```python
import jax
import jax.numpy as jnp
from jax import lax
from jax.experimental import pallas as pl
from jax.experimental.pallas import tpu as pltpu
from jax.sharding import PartitionSpec as P

MESH = pl.DeviceIdType.MESH
DT = 0.5
NZ = 16
ROWS = 16
LANES = 128
TOP = 8
END = TOP + ROWS
TILE = (8, LANES)


def fill_tables(tables, eps_ref, res_ref, damp_ref, str_ref):
    for m in range(4):
        one = jnp.ones(TILE, jnp.float32)
        inv = one if m == 3 else one / jnp.full(TILE, eps_ref[m])
        c3_sum = jnp.zeros(TILE, jnp.float32)
        r = jnp.zeros(TILE, jnp.float32)
        for k in range(2):
            res = jnp.full(TILE, res_ref[k, m])
            damp = jnp.full(TILE, damp_ref[k, m])
            gain = jnp.full(TILE, str_ref[k, m])
            if m == 3:
                gain = jnp.zeros(TILE, jnp.float32)
            w = res * res * (DT * DT)
            s = 1.0 + damp * (DT / 2.0)
            c1 = (2.0 - w) / s
            c2 = (damp * (DT / 2.0) - 1.0) / s
            c3 = gain * w / s
            g = inv * (1.0 - c1)
            h = -inv * c2
            tables[2 + k, m] = g
            tables[4 + k, m] = h
            tables[6 + k, m] = g * c1 + h
            tables[8 + k, m] = g * c2
            c3_sum = c3_sum + c3
            r = r + g * c3
        tables[0, m] = 1.0 - inv * c3_sum
        tables[1, m] = inv * DT
        tables[10, m] = r


def kernel(
    e_hbm, h_hbm, now_hbm, prev_hbm, mat_hbm, eps_hbm, res_hbm, damp_hbm, str_hbm,
    e_out, h_out,
    eps_ref, res_ref, damp_ref, str_ref,
    eh, ad, now, prev, mat, tables, keep, late, h1, e1, h2,
    strips, wide, sh1, se1, sh2, load_sem, send_sem, recv_sem,
):
    gx, gy = lax.axis_index("gx"), lax.axis_index("gy")
    nx, ny = lax.axis_size("gx"), lax.axis_size("gy")
    xp, xn = lax.rem(gx + nx - 1, nx), lax.rem(gx + 1, nx)
    yp, yn = lax.rem(gy + ny - 1, ny), lax.rem(gy + 1, ny)

    barrier = pltpu.get_barrier_semaphore()
    for d in ((xp, yp), (xp, yn), (xn, yp), (xn, yn), (gx, yp), (gx, yn), (xp, gy), (xn, gy)):
        pl.semaphore_signal(barrier, inc=1, device_id=d, device_id_type=MESH)
    loads = [
        pltpu.make_async_copy(src, dst, load_sem.at[i])
        for i, (src, dst) in enumerate((
            (e_hbm, eh.at[0:3, 1 : NZ + 1, TOP:END, :]),
            (h_hbm, eh.at[3:6, 1 : NZ + 1, TOP:END, :]),
            (mat_hbm, mat),
            (now_hbm, now),
            (prev_hbm, prev),
            (eps_hbm, eps_ref),
            (res_hbm, res_ref),
            (damp_hbm, damp_ref),
            (str_hbm, str_ref),
        ))
    ]
    for c in loads:
        c.start()
    pl.semaphore_wait(barrier, 8)

    def send(index, src, dst, device):
        c = pltpu.make_async_remote_copy(
            src_ref=src, dst_ref=dst, send_sem=send_sem.at[index], recv_sem=recv_sem.at[index],
            device_id=device, device_id_type=MESH,
        )
        c.start()
        return c

    inside = pl.ds(1, NZ)
    first = [
        send(0, e_hbm.at[:, :, 14:16, :], eh.at[0:3, inside, 6:8, :], (xn, gy)),
        send(1, h_hbm.at[:, :, 14:16, :], eh.at[3:6, inside, 6:8, :], (xn, gy)),
        send(2, e_hbm.at[:, :, 0:2, :], eh.at[0:3, inside, 24:26, :], (xp, gy)),
        send(3, h_hbm.at[:, :, 0:1, :], eh.at[3:6, inside, 24:25, :], (xp, gy)),
    ]
    zero = jnp.zeros((40, LANES), jnp.float32)
    for c in range(3):
        eh[c, NZ + 1] = zero
        e1[c, NZ] = zero
        h1[c, 0] = zero
        h2[c, 0] = zero

    lane = lax.broadcasted_iota(jnp.int32, TILE, 1)
    slot = lane & 7

    def pack(items):
        for b in (0, 8):
            rows = slice(TOP + b, TOP + b + 8)
            for tile in sorted({i // 4 for i in items}):
                group = [i for i in items if i // 4 == tile]
                right = jnp.zeros(TILE, jnp.float32)
                left = jnp.zeros(TILE, jnp.float32)
                for z in range(NZ):
                    for i in group:
                        p = 8 * z + 2 * (i % 4)
                        f = eh[i, z + 1, rows, :] if i < 6 else ad[i - 8, z, rows, :]
                        f = pltpu.roll(f, p + 2, 1)
                        right = jnp.where(lane // 2 == p // 2, f, right)
                        left = jnp.where(lane // 2 == (p // 2 + 1) % 64, f, left)
                strips[0, tile, rows, :] = right
                strips[1, tile, rows, :] = left

    loads[0].wait()
    loads[1].wait()
    pack(range(6))
    a, b = pl.ds(22, 2), pl.ds(8, 2)
    low, high = pl.ds(6, 2), pl.ds(24, 2)
    mid, part = pl.ds(TOP, ROWS), pl.ds(0, 2)
    first += [
        send(4, strips.at[0, part, a, :], strips.at[2, part, low, :], (xn, yn)),
        send(5, strips.at[1, part, a, :], strips.at[3, part, low, :], (xn, yp)),
        send(6, strips.at[0, part, b, :], strips.at[2, part, high, :], (xp, yn)),
        send(7, strips.at[1, part, b, :], strips.at[3, part, high, :], (xp, yp)),
        send(8, strips.at[0, part, mid, :], strips.at[2, part, mid, :], (gx, yn)),
        send(9, strips.at[1, part, mid, :], strips.at[3, part, mid, :], (gx, yp)),
        send(10, strips.at[0:2, part, a, :], strips.at[0:2, part, low, :], (xn, gy)),
        send(11, strips.at[0:2, part, b, :], strips.at[0:2, part, high, :], (xp, gy)),
    ]
    for c in loads[5:]:
        c.wait()
    fill_tables(tables, eps_ref, res_ref, damp_ref, str_ref)
    for c in loads[2:5]:
        c.wait()

    def local(z, _):
        for b in (0, 8):
            kind = mat[z, b : b + 8, :]
            odd = (kind & 1) == 1
            upper = kind >= 2

            def value(i):
                return jnp.where(
                    upper,
                    jnp.where(odd, tables[i, 3], tables[i, 2]),
                    jnp.where(odd, tables[i, 1], tables[i, 0]),
                )

            e, d, g0, g1, w0, w1, p0, p1, q0, q1, r = [value(i) for i in range(11)]
            rows = slice(TOP + b, TOP + b + 8)
            keep[z, b : b + 8, :] = e
            ad[3, z, rows, :] = d
            for c in range(3):
                f = eh[c, z + 1, rows, :]
                n0, n1 = now[0, c, z, b : b + 8, :], now[1, c, z, b : b + 8, :]
                m0, m1 = prev[0, c, z, b : b + 8, :], prev[1, c, z, b : b + 8, :]
                ad[c, z, rows, :] = (e * f + (g0 * n0 + g1 * n1)) + (w0 * m0 + w1 * m1)
                late[c, z, b : b + 8, :] = (r * f + (p0 * n0 + p1 * n1)) + (q0 * m0 + q1 * m1)
        return 0

    lax.fori_loop(0, NZ, local, 0, unroll=8)
    pack(range(8, 12))
    second = [
        send(12, strips.at[1, 2, pl.ds(23, 1), :], strips.at[3, 2, pl.ds(7, 1), :], (xn, yp)),
        send(13, strips.at[0, 2, pl.ds(8, 1), :], strips.at[2, 2, pl.ds(24, 1), :], (xp, yn)),
        send(14, strips.at[0, 2, mid, :], strips.at[2, 2, mid, :], (gx, yn)),
        send(15, strips.at[1, 2, mid, :], strips.at[3, 2, mid, :], (gx, yp)),
        send(16, ad.at[:, :, 23:24, :], ad.at[:, :, 7:8, :], (xn, gy)),
        send(17, ad.at[1:4, :, 8:9, :], ad.at[1:4, :, 24:25, :], (xp, gy)),
    ]

    def widen(items, starts):
        for r in starts:
            rows = slice(r, r + 8)
            for tile in sorted({i // 4 for i in items}):
                right, left = strips[0, tile, rows, :], pltpu.roll(strips[1, tile, rows, :], 4, 1)
                before, after = pltpu.roll(strips[2, tile, rows, :], 4, 1), strips[3, tile, rows, :]
                for i in items:
                    if i // 4 != tile:
                        continue
                    p = 2 * (i % 4)
                    q = (lane + 8 - p) & 7
                    f = jnp.where(q < 4, jnp.where(q < 2, right, after), jnp.where(q < 6, before, left))
                    wide[i, rows, :] = pltpu.roll(f, LANES - p, 1) if p else f

    for c in first:
        c.wait_recv()
    widen(range(6), (6, 14, 22))

    def ahead_z(f):
        return jnp.where(lane < 120, pltpu.roll(f, 120, 1), 0.0)

    def behind_z(f):
        return jnp.where(lane >= 8, pltpu.roll(f, 8, 1), 0.0)

    def h_step(ex, ey, ez, hx, hy, hz, ex_y, ez_y, ey_x, ez_x, ex_z, ey_z):
        return (
            hx - DT * ((ez_y - ez) - (ey_z - ey)),
            hy - DT * ((ex_z - ex) - (ez_x - ez)),
            hz - DT * ((ey_x - ey) - (ex_y - ex)),
        )

    def curl(hx, hy, hz, hx_y, hz_y, hy_x, hz_x, hx_z, hy_z):
        return (
            (hz - hz_y) - (hy - hy_z),
            (hx - hx_z) - (hz - hz_x),
            (hy - hy_x) - (hx - hx_y),
        )

    def strip_h(e_ref, h_ref, base, out, starts):
        for r in starts:
            rows, next_rows = slice(r, r + 8), slice(r + 1, r + 9)
            ex, ey, ez = (e_ref[i, rows, :] for i in range(3))
            new = h_step(
                ex, ey, ez, *(h_ref[base + i, rows, :] for i in range(3)),
                pltpu.roll(ex, 127, 1), pltpu.roll(ez, 127, 1),
                e_ref[1, next_rows, :], e_ref[2, next_rows, :], ahead_z(ex), ahead_z(ey),
            )
            for i in range(3):
                out[i, rows, :] = new[i]

    def main_h(e_ref, shift, h_ref, h_base, strip, out, starts):
        def body(z, _):
            far = 125 - 8 * z
            for r in starts:
                rows, next_rows = slice(r, r + 8), slice(r + 1, r + 9)
                ex, ey, ez = (e_ref[i, z + shift, rows, :] for i in range(3))
                new = h_step(
                    ex, ey, ez, *(h_ref[h_base + i, z + 1, rows, :] for i in range(3)),
                    jnp.where(lane == 127, pltpu.roll(strip[0, rows, :], far, 1), pltpu.roll(ex, 127, 1)),
                    jnp.where(lane == 127, pltpu.roll(strip[2, rows, :], far, 1), pltpu.roll(ez, 127, 1)),
                    e_ref[1, z + shift, next_rows, :], e_ref[2, z + shift, next_rows, :],
                    e_ref[0, z + shift + 1, rows, :], e_ref[1, z + shift + 1, rows, :],
                )
                for i in range(3):
                    out[i, z + 1, rows, :] = new[i]
            return 0

        lax.fori_loop(0, NZ, body, 0, unroll=NZ)

    def main_curl(h_ref, z, r, strip):
        rows, back_rows = slice(r, r + 8), slice(r - 1, r + 7)
        far = 123 - 8 * z
        hx, hy, hz = (h_ref[i, z + 1, rows, :] for i in range(3))
        return curl(
            hx, hy, hz,
            jnp.where(lane == 0, pltpu.roll(strip[0, rows, :], far, 1), pltpu.roll(hx, 1, 1)),
            jnp.where(lane == 0, pltpu.roll(strip[2, rows, :], far, 1), pltpu.roll(hz, 1, 1)),
            h_ref[1, z + 1, back_rows, :], h_ref[2, z + 1, back_rows, :],
            h_ref[0, z, rows, :], h_ref[1, z, rows, :],
        )

    strip_h(wide, wide, 3, sh1, (6, 14, 22))
    main_h(eh, 1, eh, 3, wide, h1, (6, 14, 22))
    for c in second:
        c.wait_recv()
    widen(range(8, 12), (7, 15, 23))
    for r in (7, 15, 23):
        rows, back_rows = slice(r, r + 8), slice(r - 1, r + 7)
        hx, hy, hz = (sh1[i, rows, :] for i in range(3))
        turn = curl(
            hx, hy, hz, pltpu.roll(hx, 1, 1), pltpu.roll(hz, 1, 1),
            sh1[1, back_rows, :], sh1[2, back_rows, :], behind_z(hx), behind_z(hy),
        )
        d = wide[11, rows, :]
        for i in range(3):
            se1[i, rows, :] = wide[8 + i, rows, :] + d * turn[i]
    strip_h(se1, sh1, 0, sh2, (7, 15, 23))

    def first_e(z, _):
        for r in (7, 15, 23):
            rows = slice(r, r + 8)
            turn = main_curl(h1, z, r, sh1)
            d = ad[3, z, rows, :]
            for i in range(3):
                e1[i, z, rows, :] = ad[i, z, rows, :] + d * turn[i]
        return 0

    lax.fori_loop(0, NZ, first_e, 0, unroll=NZ)
    main_h(e1, 0, h1, 0, se1, h2, (7, 15, 23))
    def second_e(z, _):
        for b in (0, 8):
            rows, here = slice(TOP + b, TOP + b + 8), slice(b, b + 8)
            turn = main_curl(h2, z, TOP + b, sh2)
            d, factor = ad[3, z, rows, :], keep[z, here, :]
            for i in range(3):
                h_out[i, z, here, :] = h2[i, z + 1, rows, :]
                e_out[i, z, here, :] = factor * e1[i, z, rows, :] + d * turn[i] + late[i, z, here, :]
        return 0

    lax.fori_loop(0, NZ, second_e, 0, unroll=NZ)
    for c in first + second:
        c.wait_send()


def write_out(e_ref, h_ref, e_out, h_out, sem):
    copies = [pltpu.make_async_copy(e_ref, e_out, sem.at[0]), pltpu.make_async_copy(h_ref, h_out, sem.at[1])]
    for c in copies:
        c.start()
    for c in copies:
        c.wait()


def body(e_field, h_field, pole_now, pole_prev, material, eps_inf, resonance, damping, strength):
    hbm = pl.BlockSpec(memory_space=pltpu.HBM)
    vmem = pl.BlockSpec(memory_space=pltpu.VMEM)
    f32 = jnp.float32
    block = pltpu.VMEM(e_field.shape, f32)
    operands = (
        e_field, h_field, pole_now, pole_prev, material,
        eps_inf, resonance.T, damping.T, strength.T,
    )
    operands = [pltpu.with_memory_space_constraint(x, pltpu.HBM) for x in operands]
    fields = pl.pallas_call(
        kernel,
        out_shape=(block, block),
        in_specs=[hbm] * 9,
        out_specs=(vmem, vmem),
        scratch_shapes=[
            pltpu.SMEM((4,), f32),
            pltpu.SMEM((2, 4), f32),
            pltpu.SMEM((2, 4), f32),
            pltpu.SMEM((2, 4), f32),
            pltpu.VMEM((6, NZ + 2, 40, LANES), f32),
            pltpu.VMEM((4, NZ, 40, LANES), f32),
            pltpu.VMEM(pole_now.shape, f32),
            pltpu.VMEM(pole_prev.shape, f32),
            pltpu.VMEM(material.shape, jnp.int32),
            pltpu.VMEM((11, 4) + TILE, f32),
            pltpu.VMEM((NZ, ROWS, LANES), f32),
            pltpu.VMEM((3, NZ, ROWS, LANES), f32),
            pltpu.VMEM((3, NZ + 1, 40, LANES), f32),
            pltpu.VMEM((3, NZ + 1, 40, LANES), f32),
            pltpu.VMEM((3, NZ + 1, 40, LANES), f32),
            pltpu.VMEM((4, 3, 40, LANES), f32),
            pltpu.VMEM((12, 40, LANES), f32),
            pltpu.VMEM((3, 40, LANES), f32),
            pltpu.VMEM((3, 40, LANES), f32),
            pltpu.VMEM((3, 40, LANES), f32),
            pltpu.SemaphoreType.DMA((9,)),
            pltpu.SemaphoreType.DMA((18,)),
            pltpu.SemaphoreType.DMA((18,)),
        ],
        compiler_params=pltpu.CompilerParams(
            collective_id=0, has_side_effects=True, vmem_limit_bytes=48 * 1024 * 1024
        ),
    )(*operands)
    fields = [pltpu.with_memory_space_constraint(x, pltpu.VMEM) for x in fields]
    return pl.pallas_call(
        write_out,
        out_shape=(pltpu.HBM(e_field.shape, f32),) * 2,
        in_specs=[vmem, vmem],
        out_specs=(hbm, hbm),
        scratch_shapes=[pltpu.SemaphoreType.DMA((2,))],
    )(*fields)


def solution(mesh):
    field = P(None, None, "gx", "gy")
    pole = P(None, None, None, "gx", "gy")
    in_specs = (field, field, pole, pole, P(None, "gx", "gy"), P(), P(), P(), P())
    return jax.shard_map(
        body, mesh=mesh, in_specs=in_specs, out_specs=(field, field), check_vma=False
    )
```

```python
import jax
import jax.numpy as jnp
from jax import lax
from jax.experimental import pallas as pl
from jax.experimental.pallas import tpu as pltpu
from jax.sharding import PartitionSpec as P

MESH = pl.DeviceIdType.MESH
DT = 0.5
NZ = 16
ROWS = 16
LANES = 128
TOP = 8
END = TOP + ROWS
TILE = (8, LANES)


def fill_tables(tables, eps_ref, res_ref, damp_ref, str_ref):
    for m in range(4):
        one = jnp.ones(TILE, jnp.float32)
        inv = one if m == 3 else one / jnp.full(TILE, eps_ref[m])
        c3_sum = jnp.zeros(TILE, jnp.float32)
        r = jnp.zeros(TILE, jnp.float32)
        for k in range(2):
            res = jnp.full(TILE, res_ref[k, m])
            damp = jnp.full(TILE, damp_ref[k, m])
            gain = jnp.full(TILE, str_ref[k, m])
            if m == 3:
                gain = jnp.zeros(TILE, jnp.float32)
            w = res * res * (DT * DT)
            s = 1.0 + damp * (DT / 2.0)
            c1 = (2.0 - w) / s
            c2 = (damp * (DT / 2.0) - 1.0) / s
            c3 = gain * w / s
            g = inv * (1.0 - c1)
            h = -inv * c2
            tables[2 + k, m] = g
            tables[4 + k, m] = h
            tables[6 + k, m] = g * c1 + h
            tables[8 + k, m] = g * c2
            c3_sum = c3_sum + c3
            r = r + g * c3
        tables[0, m] = 1.0 - inv * c3_sum
        tables[1, m] = inv * DT
        tables[10, m] = r


def kernel(
    e_hbm, h_hbm, now_hbm, prev_hbm, mat_hbm, eps_hbm, res_hbm, damp_hbm, str_hbm,
    e_out, h_out,
    eps_ref, res_ref, damp_ref, str_ref,
    eh, ad, now, prev, mat, tables, keep, late, h1, e1, h2,
    strips, wide, sh1, se1, sh2, edge_e, edge_h, edge_new, outgo, income, ring,
    load_sem, send_sem, recv_sem,
):
    gx, gy = lax.axis_index("gx"), lax.axis_index("gy")
    nx, ny = lax.axis_size("gx"), lax.axis_size("gy")
    xp, xn = lax.rem(gx + nx - 1, nx), lax.rem(gx + 1, nx)
    yp, yn = lax.rem(gy + ny - 1, ny), lax.rem(gy + 1, ny)

    barrier = pltpu.get_barrier_semaphore()
    for d in ((xp, yp), (xp, yn), (xn, yp), (xn, yn), (gx, yp), (gx, yn), (xp, gy), (xn, gy)):
        pl.semaphore_signal(barrier, inc=1, device_id=d, device_id_type=MESH)
    loads = [
        pltpu.make_async_copy(src, dst, load_sem.at[i])
        for i, (src, dst) in enumerate((
            (e_hbm, eh.at[0:3, 1 : NZ + 1, TOP:END, :]),
            (h_hbm, eh.at[3:6, 1 : NZ + 1, TOP:END, :]),
            (mat_hbm, mat),
            (now_hbm, now),
            (prev_hbm, prev),
            (eps_hbm, eps_ref),
            (res_hbm, res_ref),
            (damp_hbm, damp_ref),
            (str_hbm, str_ref),
        ))
    ] + [
        pltpu.make_async_copy(field.at[:, :, row, :], edge.at[k, :, 8:24, :], load_sem.at[9 + 4 * j + k])
        for j, (field, edge, rows) in enumerate(((e_hbm, edge_e, (0, 1, 14, 15)), (h_hbm, edge_h, (0, 14, 15))))
        for k, row in enumerate(rows)
    ]
    for c in loads:
        c.start()

    def send(index, src, dst, device):
        c = pltpu.make_async_remote_copy(
            src_ref=src, dst_ref=dst, send_sem=send_sem.at[index], recv_sem=recv_sem.at[index],
            device_id=device, device_id_type=MESH,
        )
        c.start()
        return c

    zero = jnp.zeros((40, LANES), jnp.float32)
    for c in range(3):
        eh[c, NZ + 1] = zero
        e1[c, NZ] = zero
        h1[c, 0] = zero
        h2[c, 0] = zero
        for k in range(4):
            edge_e[k, c, 24:32, :] = jnp.zeros(TILE, jnp.float32)
        for k in range(2):
            edge_new[k, c, 0:8, :] = jnp.zeros(TILE, jnp.float32)

    lane = lax.broadcasted_iota(jnp.int32, TILE, 1)
    slot = lane & 7

    def pack(items):
        for b in (0, 8):
            rows = slice(TOP + b, TOP + b + 8)
            for tile in sorted({i // 4 for i in items}):
                group = [i for i in items if i // 4 == tile]
                right = jnp.zeros(TILE, jnp.float32)
                left = jnp.zeros(TILE, jnp.float32)
                for z in range(NZ):
                    for i in group:
                        p = 8 * z + 2 * (i % 4)
                        f = eh[i, z + 1, rows, :] if i < 6 else ad[i - 8, z, rows, :]
                        f = pltpu.roll(f, p + 2, 1)
                        right = jnp.where(lane // 2 == p // 2, f, right)
                        left = jnp.where(lane // 2 == (p // 2 + 1) % 64, f, left)
                strips[0, tile, rows, :] = right
                strips[1, tile, rows, :] = left

    loads[0].wait()
    loads[1].wait()
    pack(range(6))
    for c in loads[5:9]:
        c.wait()
    fill_tables(tables, eps_ref, res_ref, damp_ref, str_ref)
    for c in loads[2:5]:
        c.wait()

    def local(z, _):
        for b in (0, 8):
            kind = mat[z, b : b + 8, :]
            odd = (kind & 1) == 1
            upper = kind >= 2

            def value(i):
                return jnp.where(
                    upper,
                    jnp.where(odd, tables[i, 3], tables[i, 2]),
                    jnp.where(odd, tables[i, 1], tables[i, 0]),
                )

            e, d, g0, g1, w0, w1, p0, p1, q0, q1, r = [value(i) for i in range(11)]
            rows = slice(TOP + b, TOP + b + 8)
            keep[z, b : b + 8, :] = e
            ad[3, z, rows, :] = d
            for c in range(3):
                f = eh[c, z + 1, rows, :]
                n0, n1 = now[0, c, z, b : b + 8, :], now[1, c, z, b : b + 8, :]
                m0, m1 = prev[0, c, z, b : b + 8, :], prev[1, c, z, b : b + 8, :]
                ad[c, z, rows, :] = (e * f + (g0 * n0 + g1 * n1)) + (w0 * m0 + w1 * m1)
                late[c, z, b : b + 8, :] = (r * f + (p0 * n0 + p1 * n1)) + (q0 * m0 + q1 * m1)
        return 0

    lax.fori_loop(0, NZ, local, 0, unroll=8)
    pack(range(8, 12))
    for c in loads[9:]:
        c.wait()

    def h_step(ex, ey, ez, hx, hy, hz, ex_y, ez_y, ey_x, ez_x, ex_z, ey_z):
        return (
            hx - DT * ((ez_y - ez) - (ey_z - ey)),
            hy - DT * ((ex_z - ex) - (ez_x - ez)),
            hz - DT * ((ey_x - ey) - (ex_y - ex)),
        )

    def curl(hx, hy, hz, hx_y, hz_y, hy_x, hz_x, hx_z, hy_z):
        return (
            (hz - hz_y) - (hy - hy_z),
            (hx - hx_z) - (hz - hz_x),
            (hy - hy_x) - (hx - hx_y),
        )

    span, up = slice(8, 24), slice(9, 25)
    down = slice(7, 23)

    def edge_step(here, there, h_here):
        e = [edge_e[here, i, span, :] for i in range(3)]
        ey_x, ez_x = (0.0, 0.0) if there is None else (edge_e[there, 1, span, :], edge_e[there, 2, span, :])
        return h_step(
            *e, *(edge_h[h_here, i, span, :] for i in range(3)),
            pltpu.roll(e[0], 127, 1), pltpu.roll(e[2], 127, 1), ey_x, ez_x,
            edge_e[here, 0, up, :], edge_e[here, 1, up, :],
        )

    end_h = edge_step(3, None, 2)
    inner_h = edge_step(2, 3, 1)
    start_h = edge_step(0, 1, 0)
    for i in range(3):
        edge_new[0, i, span, :] = end_h[i]
        edge_new[1, i, span, :] = start_h[i]
    hx, hy, hz = end_h
    turn = curl(
        hx, hy, hz, pltpu.roll(hx, 1, 1), pltpu.roll(hz, 1, 1), inner_h[1], inner_h[2],
        edge_new[0, 0, down, :], edge_new[0, 1, down, :],
    )
    d = ad[3, :, 23, :]
    outgo[0], outgo[1], outgo[5] = hy, hz, d
    for i in range(3):
        outgo[2 + i] = ad[i, :, 23, :] + d * turn[i]
    hx, hy, hz = start_h
    d = ad[3, :, 8, :]
    outgo[6] = ad[1, :, 8, :] + d * ((hx - edge_new[1, 0, down, :]) - hz)
    outgo[7] = ad[2, :, 8, :] + d * (hy - (hx - pltpu.roll(hx, 1, 1)))
    outgo[8] = d

    a, b = pl.ds(22, 2), pl.ds(8, 2)
    low, high = pl.ds(6, 2), pl.ds(24, 2)
    mid = pl.ds(TOP, ROWS)
    pl.semaphore_wait(barrier, 8)
    sends = [
        send(0, strips.at[0, :, a, :], strips.at[2, :, low, :], (xn, yn)),
        send(1, strips.at[1, :, a, :], strips.at[3, :, low, :], (xn, yp)),
        send(2, strips.at[0, :, b, :], strips.at[2, :, high, :], (xp, yn)),
        send(3, strips.at[1, :, b, :], strips.at[3, :, high, :], (xp, yp)),
        send(4, strips.at[0, :, mid, :], strips.at[2, :, mid, :], (gx, yn)),
        send(5, strips.at[1, :, mid, :], strips.at[3, :, mid, :], (gx, yp)),
        send(6, strips.at[0:2, :, a, :], strips.at[0:2, :, low, :], (xn, gy)),
        send(7, strips.at[0:2, :, b, :], strips.at[0:2, :, high, :], (xp, gy)),
        send(8, e_hbm.at[1:3, :, 0:1, :], eh.at[1:3, 1 : NZ + 1, 24:25, :], (xp, gy)),
        send(9, outgo.at[0:6], income.at[0:6], (xn, gy)),
        send(10, outgo.at[6:9], income.at[6:9], (xp, gy)),
    ]

    def widen(items, starts):
        for r in starts:
            rows = slice(r, r + 8)
            for tile in sorted({i // 4 for i in items}):
                right, left = strips[0, tile, rows, :], pltpu.roll(strips[1, tile, rows, :], 4, 1)
                before, after = pltpu.roll(strips[2, tile, rows, :], 4, 1), strips[3, tile, rows, :]
                for i in items:
                    if i // 4 != tile:
                        continue
                    p = 2 * (i % 4)
                    q = (lane + 8 - p) & 7
                    f = jnp.where(q < 4, jnp.where(q < 2, right, after), jnp.where(q < 6, before, left))
                    wide[i, rows, :] = pltpu.roll(f, LANES - p, 1) if p else f

    for c in sends:
        c.wait_recv()
    widen(range(6), (6, 14, 22))
    widen(range(8, 12), (7, 15, 23))

    def ahead_z(f):
        return jnp.where(lane < 120, pltpu.roll(f, 120, 1), 0.0)

    def behind_z(f):
        return jnp.where(lane >= 8, pltpu.roll(f, 8, 1), 0.0)

    def strip_h(e_ref, h_ref, base, out, starts):
        for r in starts:
            rows, next_rows = slice(r, r + 8), slice(r + 1, r + 9)
            ex, ey, ez = (e_ref[i, rows, :] for i in range(3))
            new = h_step(
                ex, ey, ez, *(h_ref[base + i, rows, :] for i in range(3)),
                pltpu.roll(ex, 127, 1), pltpu.roll(ez, 127, 1),
                e_ref[1, next_rows, :], e_ref[2, next_rows, :], ahead_z(ex), ahead_z(ey),
            )
            for i in range(3):
                out[i, rows, :] = new[i]

    def main_h(e_ref, shift, h_ref, h_base, strip, out, starts):
        def body(z, _):
            far = 125 - 8 * z
            for r in starts:
                rows, next_rows = slice(r, r + 8), slice(r + 1, r + 9)
                ex, ey, ez = (e_ref[i, z + shift, rows, :] for i in range(3))
                new = h_step(
                    ex, ey, ez, *(h_ref[h_base + i, z + 1, rows, :] for i in range(3)),
                    jnp.where(lane == 127, pltpu.roll(strip[0, rows, :], far, 1), pltpu.roll(ex, 127, 1)),
                    jnp.where(lane == 127, pltpu.roll(strip[2, rows, :], far, 1), pltpu.roll(ez, 127, 1)),
                    e_ref[1, z + shift, next_rows, :], e_ref[2, z + shift, next_rows, :],
                    e_ref[0, z + shift + 1, rows, :], e_ref[1, z + shift + 1, rows, :],
                )
                for i in range(3):
                    out[i, z + 1, rows, :] = new[i]
            return 0

        lax.fori_loop(0, NZ, body, 0, unroll=NZ)

    def main_curl(h_ref, z, r, strip):
        rows, back_rows = slice(r, r + 8), slice(r - 1, r + 7)
        far = 123 - 8 * z
        hx, hy, hz = (h_ref[i, z + 1, rows, :] for i in range(3))
        return curl(
            hx, hy, hz,
            jnp.where(lane == 0, pltpu.roll(strip[0, rows, :], far, 1), pltpu.roll(hx, 1, 1)),
            jnp.where(lane == 0, pltpu.roll(strip[2, rows, :], far, 1), pltpu.roll(hz, 1, 1)),
            h_ref[1, z + 1, back_rows, :], h_ref[2, z + 1, back_rows, :],
            h_ref[0, z, rows, :], h_ref[1, z, rows, :],
        )

    strip_h(wide, wide, 3, sh1, (6, 14, 22))
    for r in (7, 15, 23):
        rows, back_rows = slice(r, r + 8), slice(r - 1, r + 7)
        hx, hy, hz = (sh1[i, rows, :] for i in range(3))
        turn = curl(
            hx, hy, hz, pltpu.roll(hx, 1, 1), pltpu.roll(hz, 1, 1),
            sh1[1, back_rows, :], sh1[2, back_rows, :], behind_z(hx), behind_z(hy),
        )
        d = wide[11, rows, :]
        for i in range(3):
            se1[i, rows, :] = wide[8 + i, rows, :] + d * turn[i]
    strip_h(se1, sh1, 0, sh2, (7, 15, 23))

    line = lane[0:1, :]
    for k, r in enumerate((7, 24)):
        for i in range(3):
            f = se1[i, r : r + 1, :]
            ring[i, k : k + 1, :] = jnp.where((line & 7) == 2, pltpu.roll(f, 124, 1), f)

    def edge_lanes(f, i, k, z):
        wrapped = pltpu.roll(ring[i, k : k + 1, :], 126 - 8 * z, 1)
        return jnp.where((line == 0) | (line == 127), wrapped, f)

    main_h(eh, 1, eh, 3, wide, h1, (8, 16))
    at = slice(7, 8)
    for z in range(NZ):
        layer = slice(z, z + 1)
        dhy = DT * eh[2, z + 1, 8:9, :]
        dhz = -DT * eh[1, z + 1, 8:9, :]
        dhy_z = dhy if z == 0 else dhy - DT * eh[2, z, 8:9, :]
        h1[1, z + 1, at, :] = income[0, layer, :] + dhy
        h1[2, z + 1, at, :] = jnp.where(
            line == 127, pltpu.roll(sh1[2, at, :], 126 - 8 * z, 1), income[1, layer, :] + dhz
        )
        d = income[5, layer, :]
        ex = income[2, layer, :] + d * ((dhz - pltpu.roll(dhz, 1, 1)) - dhy_z)
        ey = income[3, layer, :] - d * dhz
        ez = income[4, layer, :] + d * dhy
        for i, f in enumerate((ex, ey, ez)):
            e1[i, z, at, :] = edge_lanes(f, i, 0, z)
        d = income[8, layer, :]
        ey = income[6, layer, :] + d * h1[2, z + 1, 23:24, :]
        ez = income[7, layer, :] - d * h1[1, z + 1, 23:24, :]
        for i, f in enumerate((ey, ez)):
            e1[i + 1, z, 24:25, :] = edge_lanes(f, i + 1, 1, z)

    def first_e(z, _):
        for r in (8, 16):
            rows = slice(r, r + 8)
            turn = main_curl(h1, z, r, sh1)
            d = ad[3, z, rows, :]
            for i in range(3):
                e1[i, z, rows, :] = ad[i, z, rows, :] + d * turn[i]
        return 0

    lax.fori_loop(0, NZ, first_e, 0, unroll=NZ)
    main_h(e1, 0, h1, 0, se1, h2, (8, 16))
    for z in range(NZ):
        ex, ey, ez = (e1[i, z, at, :] for i in range(3))
        ex_y = jnp.where(line == 127, pltpu.roll(se1[0, at, :], 125 - 8 * z, 1), pltpu.roll(ex, 127, 1))
        h2[1, z + 1, at, :] = h1[1, z + 1, at, :] - DT * ((e1[0, z + 1, at, :] - ex) - (e1[2, z, 8:9, :] - ez))
        h2[2, z + 1, at, :] = h1[2, z + 1, at, :] - DT * ((e1[1, z, 8:9, :] - ey) - (ex_y - ex))

    def second_e(z, _):
        for b in (0, 8):
            rows, here = slice(TOP + b, TOP + b + 8), slice(b, b + 8)
            turn = main_curl(h2, z, TOP + b, sh2)
            d, factor = ad[3, z, rows, :], keep[z, here, :]
            for i in range(3):
                h_out[i, z, here, :] = h2[i, z + 1, rows, :]
                e_out[i, z, here, :] = factor * e1[i, z, rows, :] + d * turn[i] + late[i, z, here, :]
        return 0

    lax.fori_loop(0, NZ, second_e, 0, unroll=NZ)
    for c in sends:
        c.wait_send()


def write_out(e_ref, h_ref, e_out, h_out, sem):
    copies = [pltpu.make_async_copy(e_ref, e_out, sem.at[0]), pltpu.make_async_copy(h_ref, h_out, sem.at[1])]
    for c in copies:
        c.start()
    for c in copies:
        c.wait()


def body(e_field, h_field, pole_now, pole_prev, material, eps_inf, resonance, damping, strength):
    hbm = pl.BlockSpec(memory_space=pltpu.HBM)
    vmem = pl.BlockSpec(memory_space=pltpu.VMEM)
    f32 = jnp.float32
    block = pltpu.VMEM(e_field.shape, f32)
    operands = (
        e_field, h_field, pole_now, pole_prev, material,
        eps_inf, resonance.T, damping.T, strength.T,
    )
    operands = [pltpu.with_memory_space_constraint(x, pltpu.HBM) for x in operands]
    fields = pl.pallas_call(
        kernel,
        out_shape=(block, block),
        in_specs=[hbm] * 9,
        out_specs=(vmem, vmem),
        scratch_shapes=[
            pltpu.SMEM((4,), f32),
            pltpu.SMEM((2, 4), f32),
            pltpu.SMEM((2, 4), f32),
            pltpu.SMEM((2, 4), f32),
            pltpu.VMEM((6, NZ + 2, 40, LANES), f32),
            pltpu.VMEM((4, NZ, 40, LANES), f32),
            pltpu.VMEM(pole_now.shape, f32),
            pltpu.VMEM(pole_prev.shape, f32),
            pltpu.VMEM(material.shape, jnp.int32),
            pltpu.VMEM((11, 4) + TILE, f32),
            pltpu.VMEM((NZ, ROWS, LANES), f32),
            pltpu.VMEM((3, NZ, ROWS, LANES), f32),
            pltpu.VMEM((3, NZ + 1, 40, LANES), f32),
            pltpu.VMEM((3, NZ + 1, 40, LANES), f32),
            pltpu.VMEM((3, NZ + 1, 40, LANES), f32),
            pltpu.VMEM((4, 3, 40, LANES), f32),
            pltpu.VMEM((12, 40, LANES), f32),
            pltpu.VMEM((3, 40, LANES), f32),
            pltpu.VMEM((3, 40, LANES), f32),
            pltpu.VMEM((3, 40, LANES), f32),
            pltpu.VMEM((4, 3, 32, LANES), f32),
            pltpu.VMEM((3, 3, 32, LANES), f32),
            pltpu.VMEM((2, 3, 32, LANES), f32),
            pltpu.VMEM((9, NZ, LANES), f32),
            pltpu.VMEM((9, NZ, LANES), f32),
            pltpu.VMEM((3, 2, LANES), f32),
            pltpu.SemaphoreType.DMA((16,)),
            pltpu.SemaphoreType.DMA((11,)),
            pltpu.SemaphoreType.DMA((11,)),
        ],
        compiler_params=pltpu.CompilerParams(
            collective_id=0, has_side_effects=True, vmem_limit_bytes=48 * 1024 * 1024
        ),
    )(*operands)
    fields = [pltpu.with_memory_space_constraint(x, pltpu.VMEM) for x in fields]
    return pl.pallas_call(
        write_out,
        out_shape=(pltpu.HBM(e_field.shape, f32),) * 2,
        in_specs=[vmem, vmem],
        out_specs=(hbm, hbm),
        scratch_shapes=[pltpu.SemaphoreType.DMA((2,))],
    )(*fields)


def solution(mesh):
    field = P(None, None, "gx", "gy")
    pole = P(None, None, None, "gx", "gy")
    in_specs = (field, field, pole, pole, P(None, "gx", "gy"), P(), P(), P(), P())
    return jax.shard_map(
        body, mesh=mesh, in_specs=in_specs, out_specs=(field, field), check_vma=False
    )
```

```python
import jax
import jax.numpy as jnp
from jax import lax
from jax.experimental import pallas as pl
from jax.experimental.pallas import tpu as pltpu
from jax.sharding import PartitionSpec as P

MESH = pl.DeviceIdType.MESH
DT = 0.5
NZ = 16
ROWS = 16
LANES = 128
TOP = 8
END = TOP + ROWS
TILE = (8, LANES)


def fill_tables(tables, eps_ref, res_ref, damp_ref, str_ref):
    for m in range(4):
        one = jnp.ones(TILE, jnp.float32)
        inv = one if m == 3 else one / jnp.full(TILE, eps_ref[m])
        c3_sum = jnp.zeros(TILE, jnp.float32)
        r = jnp.zeros(TILE, jnp.float32)
        for k in range(2):
            res = jnp.full(TILE, res_ref[k, m])
            damp = jnp.full(TILE, damp_ref[k, m])
            gain = jnp.full(TILE, str_ref[k, m])
            if m == 3:
                gain = jnp.zeros(TILE, jnp.float32)
            w = res * res * (DT * DT)
            s = 1.0 + damp * (DT / 2.0)
            c1 = (2.0 - w) / s
            c2 = (damp * (DT / 2.0) - 1.0) / s
            c3 = gain * w / s
            g = inv * (1.0 - c1)
            h = -inv * c2
            tables[2 + k, m] = g
            tables[4 + k, m] = h
            tables[6 + k, m] = g * c1 + h
            tables[8 + k, m] = g * c2
            c3_sum = c3_sum + c3
            r = r + g * c3
        tables[0, m] = 1.0 - inv * c3_sum
        tables[1, m] = inv * DT
        tables[10, m] = r


def kernel(
    e_hbm, h_hbm, now_hbm, prev_hbm, mat_hbm, eps_hbm, res_hbm, damp_hbm, str_hbm,
    e_out, h_out,
    eps_ref, res_ref, damp_ref, str_ref,
    eh, ad, now, prev, mat, tables, keep, late, h1, e1, h2,
    strips, wide, sh1, se1, sh2, edge_e, edge_h, edge_new, outgo, income, fix,
    load_sem, send_sem, recv_sem,
):
    gx, gy = lax.axis_index("gx"), lax.axis_index("gy")
    nx, ny = lax.axis_size("gx"), lax.axis_size("gy")
    xp, xn = lax.rem(gx + nx - 1, nx), lax.rem(gx + 1, nx)
    yp, yn = lax.rem(gy + ny - 1, ny), lax.rem(gy + 1, ny)

    barrier = pltpu.get_barrier_semaphore()
    for d in ((xp, yp), (xp, yn), (xn, yp), (xn, yn), (gx, yp), (gx, yn), (xp, gy), (xn, gy)):
        pl.semaphore_signal(barrier, inc=1, device_id=d, device_id_type=MESH)
    loads = [
        pltpu.make_async_copy(src, dst, load_sem.at[i])
        for i, (src, dst) in enumerate((
            (e_hbm, eh.at[0:3, 1 : NZ + 1, TOP:END, :]),
            (h_hbm, eh.at[3:6, 1 : NZ + 1, TOP:END, :]),
            (mat_hbm, mat),
            (now_hbm, now),
            (prev_hbm, prev),
            (eps_hbm, eps_ref),
            (res_hbm, res_ref),
            (damp_hbm, damp_ref),
            (str_hbm, str_ref),
        ))
    ] + [
        pltpu.make_async_copy(field.at[:, :, row, :], edge.at[k, :, 8:24, :], load_sem.at[9 + 4 * j + k])
        for j, (field, edge, rows) in enumerate(((e_hbm, edge_e, (0, 1, 14, 15)), (h_hbm, edge_h, (0, 14, 15))))
        for k, row in enumerate(rows)
    ]
    for c in loads:
        c.start()

    def send(index, src, dst, device):
        c = pltpu.make_async_remote_copy(
            src_ref=src, dst_ref=dst, send_sem=send_sem.at[index], recv_sem=recv_sem.at[index],
            device_id=device, device_id_type=MESH,
        )
        c.start()
        return c

    zero = jnp.zeros((40, LANES), jnp.float32)
    for c in range(3):
        eh[c, NZ + 1] = zero
        e1[c, NZ] = zero
        h1[c, 0] = zero
        h2[c, 0] = zero
        for k in range(4):
            edge_e[k, c, 0:8, :] = jnp.zeros(TILE, jnp.float32)
            edge_e[k, c, 24:32, :] = jnp.zeros(TILE, jnp.float32)
        for k in range(2):
            edge_new[k, c, 0:8, :] = jnp.zeros(TILE, jnp.float32)

    lane = lax.broadcasted_iota(jnp.int32, TILE, 1)
    slot = lane & 7

    def pack(items):
        for b in (0, 8):
            rows = slice(TOP + b, TOP + b + 8)
            for tile in sorted({i // 4 for i in items}):
                group = [i for i in items if i // 4 == tile]
                right = jnp.zeros(TILE, jnp.float32)
                left = jnp.zeros(TILE, jnp.float32)
                for z in range(NZ):
                    for i in group:
                        p = 8 * z + 2 * (i % 4)
                        f = eh[i, z + 1, rows, :] if i < 6 else ad[i - 8, z, rows, :]
                        f = pltpu.roll(f, p + 2, 1)
                        right = jnp.where(lane // 2 == p // 2, f, right)
                        left = jnp.where(lane // 2 == (p // 2 + 1) % 64, f, left)
                strips[0, tile, rows, :] = right
                strips[1, tile, rows, :] = left

    loads[0].wait()
    loads[1].wait()
    pack(range(6))
    for c in loads[5:9]:
        c.wait()
    fill_tables(tables, eps_ref, res_ref, damp_ref, str_ref)
    for c in loads[2:5]:
        c.wait()

    def local(z, _):
        for b in (0, 8):
            kind = mat[z, b : b + 8, :]
            odd = (kind & 1) == 1
            upper = kind >= 2

            def value(i):
                return jnp.where(
                    upper,
                    jnp.where(odd, tables[i, 3], tables[i, 2]),
                    jnp.where(odd, tables[i, 1], tables[i, 0]),
                )

            e, d, g0, g1, w0, w1, p0, p1, q0, q1, r = [value(i) for i in range(11)]
            rows = slice(TOP + b, TOP + b + 8)
            keep[z, b : b + 8, :] = e
            ad[3, z, rows, :] = d
            for c in range(3):
                f = eh[c, z + 1, rows, :]
                n0, n1 = now[0, c, z, b : b + 8, :], now[1, c, z, b : b + 8, :]
                m0, m1 = prev[0, c, z, b : b + 8, :], prev[1, c, z, b : b + 8, :]
                ad[c, z, rows, :] = (e * f + (g0 * n0 + g1 * n1)) + (w0 * m0 + w1 * m1)
                late[c, z, b : b + 8, :] = (r * f + (p0 * n0 + p1 * n1)) + (q0 * m0 + q1 * m1)
        return 0

    lax.fori_loop(0, NZ, local, 0, unroll=NZ)
    pack(range(8, 12))
    for c in loads[9:]:
        c.wait()

    def h_step(ex, ey, ez, hx, hy, hz, ex_y, ez_y, ey_x, ez_x, ex_z, ey_z):
        return (
            hx - DT * ((ez_y - ez) - (ey_z - ey)),
            hy - DT * ((ex_z - ex) - (ez_x - ez)),
            hz - DT * ((ey_x - ey) - (ex_y - ex)),
        )

    def curl(hx, hy, hz, hx_y, hz_y, hy_x, hz_x, hx_z, hy_z):
        return (
            (hz - hz_y) - (hy - hy_z),
            (hx - hx_z) - (hz - hz_x),
            (hy - hy_x) - (hx - hx_y),
        )

    span, up = slice(8, 24), slice(9, 25)
    down = slice(7, 23)

    def edge_step(here, there, h_here):
        e = [edge_e[here, i, span, :] for i in range(3)]
        ey_x, ez_x = (0.0, 0.0) if there is None else (edge_e[there, 1, span, :], edge_e[there, 2, span, :])
        return h_step(
            *e, *(edge_h[h_here, i, span, :] for i in range(3)),
            pltpu.roll(e[0], 127, 1), pltpu.roll(e[2], 127, 1), ey_x, ez_x,
            edge_e[here, 0, up, :], edge_e[here, 1, up, :],
        )

    end_h = edge_step(3, None, 2)
    inner_h = edge_step(2, 3, 1)
    start_h = edge_step(0, 1, 0)
    for i in range(3):
        edge_new[0, i, span, :] = end_h[i]
        edge_new[1, i, span, :] = start_h[i]
    hx, hy, hz = end_h
    turn = curl(
        hx, hy, hz, pltpu.roll(hx, 1, 1), pltpu.roll(hz, 1, 1), inner_h[1], inner_h[2],
        edge_new[0, 0, down, :], edge_new[0, 1, down, :],
    )
    d = ad[3, :, 23, :]
    outgo[0], outgo[1], outgo[5] = hy, hz, d
    for i in range(3):
        outgo[2 + i] = ad[i, :, 23, :] + d * turn[i]
    hx, hy, hz = start_h
    d = ad[3, :, 8, :]
    outgo[6] = ad[1, :, 8, :] + d * ((hx - edge_new[1, 0, down, :]) - hz)
    outgo[7] = ad[2, :, 8, :] + d * (hy - (hx - pltpu.roll(hx, 1, 1)))
    outgo[8] = d

    fix[0] = DT * edge_e[0, 2, span, :]
    dhz = -DT * edge_e[0, 1, span, :]
    fix[1] = dhz
    fix[2] = (dhz - pltpu.roll(dhz, 1, 1)) - (fix[0] - DT * edge_e[0, 2, down, :])

    a, b = pl.ds(22, 2), pl.ds(8, 2)
    low, high = pl.ds(6, 2), pl.ds(24, 2)
    mid = pl.ds(TOP, ROWS)
    pl.semaphore_wait(barrier, 8)
    sends = [
        send(0, strips.at[0, :, a, :], strips.at[2, :, low, :], (xn, yn)),
        send(1, strips.at[1, :, a, :], strips.at[3, :, low, :], (xn, yp)),
        send(2, strips.at[0, :, b, :], strips.at[2, :, high, :], (xp, yn)),
        send(3, strips.at[1, :, b, :], strips.at[3, :, high, :], (xp, yp)),
        send(4, strips.at[0, :, mid, :], strips.at[2, :, mid, :], (gx, yn)),
        send(5, strips.at[1, :, mid, :], strips.at[3, :, mid, :], (gx, yp)),
        send(6, strips.at[0:2, :, a, :], strips.at[0:2, :, low, :], (xn, gy)),
        send(7, strips.at[0:2, :, b, :], strips.at[0:2, :, high, :], (xp, gy)),
        send(8, e_hbm.at[1:3, :, 0:1, :], eh.at[1:3, 1 : NZ + 1, 24:25, :], (xp, gy)),
        send(9, outgo.at[0:6], income.at[0:6], (xn, gy)),
        send(10, outgo.at[6:9], income.at[6:9], (xp, gy)),
    ]

    def widen(items, starts):
        for r in starts:
            rows = slice(r, r + 8)
            for tile in sorted({i // 4 for i in items}):
                right, left = strips[0, tile, rows, :], pltpu.roll(strips[1, tile, rows, :], 4, 1)
                before, after = pltpu.roll(strips[2, tile, rows, :], 4, 1), strips[3, tile, rows, :]
                for i in items:
                    if i // 4 != tile:
                        continue
                    p = 2 * (i % 4)
                    q = (lane + 8 - p) & 7
                    f = jnp.where(q < 4, jnp.where(q < 2, right, after), jnp.where(q < 6, before, left))
                    wide[i, rows, :] = pltpu.roll(f, LANES - p, 1) if p else f


    def ahead_z(f):
        return jnp.where(lane < 120, pltpu.roll(f, 120, 1), 0.0)

    def behind_z(f):
        return jnp.where(lane >= 8, pltpu.roll(f, 8, 1), 0.0)

    def strip_h(e_ref, h_ref, base, out, starts):
        for r in starts:
            rows, next_rows = slice(r, r + 8), slice(r + 1, r + 9)
            ex, ey, ez = (e_ref[i, rows, :] for i in range(3))
            new = h_step(
                ex, ey, ez, *(h_ref[base + i, rows, :] for i in range(3)),
                pltpu.roll(ex, 127, 1), pltpu.roll(ez, 127, 1),
                e_ref[1, next_rows, :], e_ref[2, next_rows, :], ahead_z(ex), ahead_z(ey),
            )
            for i in range(3):
                out[i, rows, :] = new[i]

    def main_h(e_ref, shift, h_ref, h_base, strip, out, starts):
        def body(z, _):
            far = 125 - 8 * z
            for r in starts:
                rows, next_rows = slice(r, r + 8), slice(r + 1, r + 9)
                ex, ey, ez = (e_ref[i, z + shift, rows, :] for i in range(3))
                new = h_step(
                    ex, ey, ez, *(h_ref[h_base + i, z + 1, rows, :] for i in range(3)),
                    jnp.where(lane == 127, pltpu.roll(strip[0, rows, :], far, 1), pltpu.roll(ex, 127, 1)),
                    jnp.where(lane == 127, pltpu.roll(strip[2, rows, :], far, 1), pltpu.roll(ez, 127, 1)),
                    e_ref[1, z + shift, next_rows, :], e_ref[2, z + shift, next_rows, :],
                    e_ref[0, z + shift + 1, rows, :], e_ref[1, z + shift + 1, rows, :],
                )
                for i in range(3):
                    out[i, z + 1, rows, :] = new[i]
            return 0

        lax.fori_loop(0, NZ, body, 0, unroll=NZ)

    def main_curl(h_ref, z, r, strip):
        rows, back_rows = slice(r, r + 8), slice(r - 1, r + 7)
        far = 123 - 8 * z
        hx, hy, hz = (h_ref[i, z + 1, rows, :] for i in range(3))
        return curl(
            hx, hy, hz,
            jnp.where(lane == 0, pltpu.roll(strip[0, rows, :], far, 1), pltpu.roll(hx, 1, 1)),
            jnp.where(lane == 0, pltpu.roll(strip[2, rows, :], far, 1), pltpu.roll(hz, 1, 1)),
            h_ref[1, z + 1, back_rows, :], h_ref[2, z + 1, back_rows, :],
            h_ref[0, z, rows, :], h_ref[1, z, rows, :],
        )

    for c in (sends[4], sends[5], sends[8]):
        c.wait_recv()
    widen((0, 2), (8, 16))
    main_h(eh, 1, eh, 3, wide, h1, (8, 16))
    for c in sends[0:4] + sends[6:8] + sends[9:]:
        c.wait_recv()
    widen(range(6), (6, 14, 22))
    widen(range(8, 12), (7, 15, 23))
    strip_h(wide, wide, 3, sh1, (6, 14, 22))
    for r in (7, 15, 23):
        rows, back_rows = slice(r, r + 8), slice(r - 1, r + 7)
        hx, hy, hz = (sh1[i, rows, :] for i in range(3))
        turn = curl(
            hx, hy, hz, pltpu.roll(hx, 1, 1), pltpu.roll(hz, 1, 1),
            sh1[1, back_rows, :], sh1[2, back_rows, :], behind_z(hx), behind_z(hy),
        )
        d = wide[11, rows, :]
        for i in range(3):
            se1[i, rows, :] = wide[8 + i, rows, :] + d * turn[i]
    strip_h(se1, sh1, 0, sh2, (7, 15, 23))

    column = lax.broadcasted_iota(jnp.int32, (NZ, LANES), 1)
    start = 8 * lax.broadcasted_iota(jnp.int32, (NZ, LANES), 0)

    def pick(f, q):
        f = jnp.broadcast_to(f, (NZ, LANES))
        return jnp.sum(jnp.where(column == start + q, f, 0.0), axis=1, keepdims=True)

    def edge_lanes(f, i, row):
        line = se1[i, row : row + 1, :]
        return jnp.where(column == 127, pick(line, 1), jnp.where(column == 0, pick(line, 6), f))

    at, layers, shifted = slice(7, 8), slice(0, NZ), slice(1, NZ + 1)
    hy_row = income[0] + fix[0]
    hz_row = jnp.where(column == 127, pick(sh1[2, at, :], 1), income[1] + fix[1])
    d = income[5]
    e_row = [
        edge_lanes(f, i, 7)
        for i, f in enumerate((income[2] + d * fix[2], income[3] - d * fix[1], income[4] + d * fix[0]))
    ]
    h1[1, shifted, 7, :] = hy_row
    h1[2, shifted, 7, :] = hz_row
    for i in range(3):
        e1[i, layers, 7, :] = e_row[i]
    d = income[8]
    e1[1, layers, 24, :] = edge_lanes(income[6] + d * h1[2, shifted, 23, :], 1, 24)
    e1[2, layers, 24, :] = edge_lanes(income[7] - d * h1[1, shifted, 23, :], 2, 24)

    def first_e(z, _):
        for r in (8, 16):
            rows = slice(r, r + 8)
            turn = main_curl(h1, z, r, sh1)
            d = ad[3, z, rows, :]
            for i in range(3):
                e1[i, z, rows, :] = ad[i, z, rows, :] + d * turn[i]
        return 0

    lax.fori_loop(0, NZ, first_e, 0, unroll=NZ)
    main_h(e1, 0, h1, 0, se1, h2, (8, 16))
    ex, ey, ez = e_row
    ex_y = jnp.where(column == 127, pick(se1[0, at, :], 2), pltpu.roll(ex, 127, 1))
    h2[1, shifted, 7, :] = hy_row - DT * ((e1[0, shifted, 7, :] - ex) - (e1[2, layers, 8, :] - ez))
    h2[2, shifted, 7, :] = hz_row - DT * ((e1[1, layers, 8, :] - ey) - (ex_y - ex))

    def second_e(z, _):
        for b in (0, 8):
            rows, here = slice(TOP + b, TOP + b + 8), slice(b, b + 8)
            turn = main_curl(h2, z, TOP + b, sh2)
            d, factor = ad[3, z, rows, :], keep[z, here, :]
            for i in range(3):
                h_out[i, z, here, :] = h2[i, z + 1, rows, :]
                e_out[i, z, here, :] = factor * e1[i, z, rows, :] + d * turn[i] + late[i, z, here, :]
        return 0

    lax.fori_loop(0, NZ, second_e, 0, unroll=NZ)
    for c in sends:
        c.wait_send()


def write_out(e_ref, h_ref, e_out, h_out, sem):
    copies = [pltpu.make_async_copy(e_ref, e_out, sem.at[0]), pltpu.make_async_copy(h_ref, h_out, sem.at[1])]
    for c in copies:
        c.start()
    for c in copies:
        c.wait()


def body(e_field, h_field, pole_now, pole_prev, material, eps_inf, resonance, damping, strength):
    hbm = pl.BlockSpec(memory_space=pltpu.HBM)
    vmem = pl.BlockSpec(memory_space=pltpu.VMEM)
    f32 = jnp.float32
    block = pltpu.VMEM(e_field.shape, f32)
    operands = (
        e_field, h_field, pole_now, pole_prev, material,
        eps_inf, resonance.T, damping.T, strength.T,
    )
    operands = [pltpu.with_memory_space_constraint(x, pltpu.HBM) for x in operands]
    fields = pl.pallas_call(
        kernel,
        out_shape=(block, block),
        in_specs=[hbm] * 9,
        out_specs=(vmem, vmem),
        scratch_shapes=[
            pltpu.SMEM((4,), f32),
            pltpu.SMEM((2, 4), f32),
            pltpu.SMEM((2, 4), f32),
            pltpu.SMEM((2, 4), f32),
            pltpu.VMEM((6, NZ + 2, 40, LANES), f32),
            pltpu.VMEM((4, NZ, 40, LANES), f32),
            pltpu.VMEM(pole_now.shape, f32),
            pltpu.VMEM(pole_prev.shape, f32),
            pltpu.VMEM(material.shape, jnp.int32),
            pltpu.VMEM((11, 4) + TILE, f32),
            pltpu.VMEM((NZ, ROWS, LANES), f32),
            pltpu.VMEM((3, NZ, ROWS, LANES), f32),
            pltpu.VMEM((3, NZ + 1, 40, LANES), f32),
            pltpu.VMEM((3, NZ + 1, 40, LANES), f32),
            pltpu.VMEM((3, NZ + 1, 40, LANES), f32),
            pltpu.VMEM((4, 3, 40, LANES), f32),
            pltpu.VMEM((12, 40, LANES), f32),
            pltpu.VMEM((3, 40, LANES), f32),
            pltpu.VMEM((3, 40, LANES), f32),
            pltpu.VMEM((3, 40, LANES), f32),
            pltpu.VMEM((4, 3, 32, LANES), f32),
            pltpu.VMEM((3, 3, 32, LANES), f32),
            pltpu.VMEM((2, 3, 32, LANES), f32),
            pltpu.VMEM((9, NZ, LANES), f32),
            pltpu.VMEM((9, NZ, LANES), f32),
            pltpu.VMEM((3, NZ, LANES), f32),
            pltpu.SemaphoreType.DMA((16,)),
            pltpu.SemaphoreType.DMA((11,)),
            pltpu.SemaphoreType.DMA((11,)),
        ],
        compiler_params=pltpu.CompilerParams(
            collective_id=0, has_side_effects=True, vmem_limit_bytes=48 * 1024 * 1024
        ),
    )(*operands)
    fields = [pltpu.with_memory_space_constraint(x, pltpu.VMEM) for x in fields]
    return pl.pallas_call(
        write_out,
        out_shape=(pltpu.HBM(e_field.shape, f32),) * 2,
        in_specs=[vmem, vmem],
        out_specs=(hbm, hbm),
        scratch_shapes=[pltpu.SemaphoreType.DMA((2,))],
    )(*fields)


def solution(mesh):
    field = P(None, None, "gx", "gy")
    pole = P(None, None, None, "gx", "gy")
    in_specs = (field, field, pole, pole, P(None, "gx", "gy"), P(), P(), P(), P())
    return jax.shard_map(
        body, mesh=mesh, in_specs=in_specs, out_specs=(field, field), check_vma=False
    )
```

```python
import jax
import jax.numpy as jnp
from jax import lax
from jax.experimental import pallas as pl
from jax.experimental.pallas import tpu as pltpu
from jax.sharding import PartitionSpec as P

MESH = pl.DeviceIdType.MESH
DT = 0.5
NZ = 16
ROWS = 16
LANES = 128
TOP = 8
END = TOP + ROWS
TILE = (8, LANES)


def fill_tables(tables, eps_ref, res_ref, damp_ref, str_ref):
    for m in range(4):
        one = jnp.ones(TILE, jnp.float32)
        inv = one if m == 3 else one / jnp.full(TILE, eps_ref[m])
        c3_sum = jnp.zeros(TILE, jnp.float32)
        r = jnp.zeros(TILE, jnp.float32)
        for k in range(2):
            res = jnp.full(TILE, res_ref[k, m])
            damp = jnp.full(TILE, damp_ref[k, m])
            gain = jnp.full(TILE, str_ref[k, m])
            if m == 3:
                gain = jnp.zeros(TILE, jnp.float32)
            w = res * res * (DT * DT)
            s = 1.0 + damp * (DT / 2.0)
            c1 = (2.0 - w) / s
            c2 = (damp * (DT / 2.0) - 1.0) / s
            c3 = gain * w / s
            g = inv * (1.0 - c1)
            h = -inv * c2
            tables[2 + k, m] = g
            tables[4 + k, m] = h
            tables[6 + k, m] = g * c1 + h
            tables[8 + k, m] = g * c2
            c3_sum = c3_sum + c3
            r = r + g * c3
        tables[0, m] = 1.0 - inv * c3_sum
        tables[1, m] = inv * DT
        tables[10, m] = r


def kernel(
    e_hbm, h_hbm, now_hbm, prev_hbm, mat_hbm, eps_hbm, res_hbm, damp_hbm, str_hbm,
    e_out, h_out,
    eps_ref, res_ref, damp_ref, str_ref,
    eh, ad, now, prev, mat, tables, keep, late, h1, e1, h2,
    strips, wide, sh1, se1, sh2, edge_e, edge_h, edge_new, outgo, income, fix,
    load_sem, send_sem, recv_sem,
):
    gx, gy = lax.axis_index("gx"), lax.axis_index("gy")
    nx, ny = lax.axis_size("gx"), lax.axis_size("gy")
    xp, xn = lax.rem(gx + nx - 1, nx), lax.rem(gx + 1, nx)
    yp, yn = lax.rem(gy + ny - 1, ny), lax.rem(gy + 1, ny)

    barrier = pltpu.get_barrier_semaphore()
    for d in ((xp, yp), (xp, yn), (xn, yp), (xn, yn), (gx, yp), (gx, yn), (xp, gy), (xn, gy)):
        pl.semaphore_signal(barrier, inc=1, device_id=d, device_id_type=MESH)
    loads = [
        pltpu.make_async_copy(src, dst, load_sem.at[i])
        for i, (src, dst) in enumerate((
            (e_hbm, eh.at[0:3, 1 : NZ + 1, TOP:END, :]),
            (h_hbm, eh.at[3:6, 1 : NZ + 1, TOP:END, :]),
            (mat_hbm, mat),
            (now_hbm, now),
            (prev_hbm, prev),
            (eps_hbm, eps_ref),
            (res_hbm, res_ref),
            (damp_hbm, damp_ref),
            (str_hbm, str_ref),
        ))
    ] + [
        pltpu.make_async_copy(field.at[:, :, row, :], edge.at[k, :, 8:24, :], load_sem.at[9 + 4 * j + k])
        for j, (field, edge, rows) in enumerate(((e_hbm, edge_e, (0, 1, 14, 15)), (h_hbm, edge_h, (0, 14, 15))))
        for k, row in enumerate(rows)
    ]
    for c in loads:
        c.start()

    def send(index, src, dst, device):
        c = pltpu.make_async_remote_copy(
            src_ref=src, dst_ref=dst, send_sem=send_sem.at[index], recv_sem=recv_sem.at[index],
            device_id=device, device_id_type=MESH,
        )
        c.start()
        return c

    zero = jnp.zeros((40, LANES), jnp.float32)
    for c in range(3):
        eh[c, NZ + 1] = zero
        e1[c, NZ] = zero
        h1[c, 0] = zero
        h2[c, 0] = zero
        for k in range(4):
            edge_e[k, c, 0:8, :] = jnp.zeros(TILE, jnp.float32)
            edge_e[k, c, 24:32, :] = jnp.zeros(TILE, jnp.float32)
        for k in range(2):
            edge_new[k, c, 0:8, :] = jnp.zeros(TILE, jnp.float32)

    lane = lax.broadcasted_iota(jnp.int32, TILE, 1)
    slot = lane & 7

    def pack(items):
        for b in (0, 8):
            rows = slice(TOP + b, TOP + b + 8)
            for tile in sorted({i // 4 for i in items}):
                group = [i for i in items if i // 4 == tile]
                right = jnp.zeros(TILE, jnp.float32)
                left = jnp.zeros(TILE, jnp.float32)
                for z in range(NZ):
                    for i in group:
                        p = 8 * z + 2 * (i % 4)
                        f = eh[i, z + 1, rows, :] if i < 6 else ad[i - 8, z, rows, :]
                        f = pltpu.roll(f, p + 2, 1)
                        right = jnp.where(lane // 2 == p // 2, f, right)
                        left = jnp.where(lane // 2 == (p // 2 + 1) % 64, f, left)
                strips[0, tile, rows, :] = right
                strips[1, tile, rows, :] = left

    loads[0].wait()
    loads[1].wait()
    pack(range(6))
    for c in loads[5:9]:
        c.wait()
    fill_tables(tables, eps_ref, res_ref, damp_ref, str_ref)
    for c in loads[2:5]:
        c.wait()

    def local(z, _):
        for b in (0, 8):
            kind = mat[z, b : b + 8, :]
            odd = (kind & 1) == 1
            upper = kind >= 2

            def value(i):
                return jnp.where(
                    upper,
                    jnp.where(odd, tables[i, 3], tables[i, 2]),
                    jnp.where(odd, tables[i, 1], tables[i, 0]),
                )

            e, d, g0, g1, w0, w1, p0, p1, q0, q1, r = [value(i) for i in range(11)]
            rows = slice(TOP + b, TOP + b + 8)
            keep[z, b : b + 8, :] = e
            ad[3, z, rows, :] = d
            for c in range(3):
                f = eh[c, z + 1, rows, :]
                n0, n1 = now[0, c, z, b : b + 8, :], now[1, c, z, b : b + 8, :]
                m0, m1 = prev[0, c, z, b : b + 8, :], prev[1, c, z, b : b + 8, :]
                ad[c, z, rows, :] = (e * f + (g0 * n0 + g1 * n1)) + (w0 * m0 + w1 * m1)
                late[c, z, b : b + 8, :] = (r * f + (p0 * n0 + p1 * n1)) + (q0 * m0 + q1 * m1)
        return 0

    lax.fori_loop(0, NZ, local, 0, unroll=NZ)
    pack(range(8, 12))
    for c in loads[9:]:
        c.wait()

    def h_step(ex, ey, ez, hx, hy, hz, ex_y, ez_y, ey_x, ez_x, ex_z, ey_z):
        return (
            hx - DT * ((ez_y - ez) - (ey_z - ey)),
            hy - DT * ((ex_z - ex) - (ez_x - ez)),
            hz - DT * ((ey_x - ey) - (ex_y - ex)),
        )

    def curl(hx, hy, hz, hx_y, hz_y, hy_x, hz_x, hx_z, hy_z):
        return (
            (hz - hz_y) - (hy - hy_z),
            (hx - hx_z) - (hz - hz_x),
            (hy - hy_x) - (hx - hx_y),
        )

    span, up = slice(8, 24), slice(9, 25)
    down = slice(7, 23)

    def edge_step(here, there, h_here):
        e = [edge_e[here, i, span, :] for i in range(3)]
        ey_x, ez_x = (0.0, 0.0) if there is None else (edge_e[there, 1, span, :], edge_e[there, 2, span, :])
        return h_step(
            *e, *(edge_h[h_here, i, span, :] for i in range(3)),
            pltpu.roll(e[0], 127, 1), pltpu.roll(e[2], 127, 1), ey_x, ez_x,
            edge_e[here, 0, up, :], edge_e[here, 1, up, :],
        )

    end_h = edge_step(3, None, 2)
    inner_h = edge_step(2, 3, 1)
    start_h = edge_step(0, 1, 0)
    for i in range(3):
        edge_new[0, i, span, :] = end_h[i]
        edge_new[1, i, span, :] = start_h[i]
    hx, hy, hz = end_h
    turn = curl(
        hx, hy, hz, pltpu.roll(hx, 1, 1), pltpu.roll(hz, 1, 1), inner_h[1], inner_h[2],
        edge_new[0, 0, down, :], edge_new[0, 1, down, :],
    )
    d = ad[3, :, 23, :]
    outgo[0], outgo[1], outgo[5] = hy, hz, d
    for i in range(3):
        outgo[2 + i] = ad[i, :, 23, :] + d * turn[i]
    hx, hy, hz = start_h
    d = ad[3, :, 8, :]
    outgo[6] = ad[1, :, 8, :] + d * ((hx - edge_new[1, 0, down, :]) - hz)
    outgo[7] = ad[2, :, 8, :] + d * (hy - (hx - pltpu.roll(hx, 1, 1)))
    outgo[8] = d

    fix[0] = DT * edge_e[0, 2, span, :]
    dhz = -DT * edge_e[0, 1, span, :]
    fix[1] = dhz
    fix[2] = (dhz - pltpu.roll(dhz, 1, 1)) - (fix[0] - DT * edge_e[0, 2, down, :])

    a, b = pl.ds(22, 2), pl.ds(8, 2)
    low, high = pl.ds(6, 2), pl.ds(24, 2)
    mid = pl.ds(TOP, ROWS)
    pl.semaphore_wait(barrier, 8)
    sends = [
        send(0, strips.at[0, 0:2, a, :], strips.at[2, 0:2, low, :], (xn, yn)),
        send(1, strips.at[1, :, a, :], strips.at[3, :, low, :], (xn, yp)),
        send(2, strips.at[0, :, b, :], strips.at[2, :, high, :], (xp, yn)),
        send(3, strips.at[1, 0:2, b, :], strips.at[3, 0:2, high, :], (xp, yp)),
        send(4, strips.at[0, :, mid, :], strips.at[2, :, mid, :], (gx, yn)),
        send(5, strips.at[1, :, mid, :], strips.at[3, :, mid, :], (gx, yp)),
        send(6, strips.at[0:2, :, a, :], strips.at[0:2, :, low, :], (xn, gy)),
        send(7, strips.at[0:2, :, b, :], strips.at[0:2, :, high, :], (xp, gy)),
        send(8, e_hbm.at[1:3, :, 0:1, :], eh.at[1:3, 1 : NZ + 1, 24:25, :], (xp, gy)),
        send(9, outgo.at[0:6], income.at[0:6], (xn, gy)),
        send(10, outgo.at[6:9], income.at[6:9], (xp, gy)),
    ]

    def widen(items, starts):
        for r in starts:
            rows = slice(r, r + 8)
            for tile in sorted({i // 4 for i in items}):
                right, left = strips[0, tile, rows, :], pltpu.roll(strips[1, tile, rows, :], 4, 1)
                before, after = pltpu.roll(strips[2, tile, rows, :], 4, 1), strips[3, tile, rows, :]
                for i in items:
                    if i // 4 != tile:
                        continue
                    p = 2 * (i % 4)
                    q = (lane + 8 - p) & 7
                    f = jnp.where(q < 4, jnp.where(q < 2, right, after), jnp.where(q < 6, before, left))
                    wide[i, rows, :] = pltpu.roll(f, LANES - p, 1) if p else f


    def ahead_z(f):
        return jnp.where(lane < 120, pltpu.roll(f, 120, 1), 0.0)

    def behind_z(f):
        return jnp.where(lane >= 8, pltpu.roll(f, 8, 1), 0.0)

    def strip_h(e_ref, h_ref, base, out, starts):
        for r in starts:
            rows, next_rows = slice(r, r + 8), slice(r + 1, r + 9)
            ex, ey, ez = (e_ref[i, rows, :] for i in range(3))
            new = h_step(
                ex, ey, ez, *(h_ref[base + i, rows, :] for i in range(3)),
                pltpu.roll(ex, 127, 1), pltpu.roll(ez, 127, 1),
                e_ref[1, next_rows, :], e_ref[2, next_rows, :], ahead_z(ex), ahead_z(ey),
            )
            for i in range(3):
                out[i, rows, :] = new[i]

    def main_h(e_ref, shift, h_ref, h_base, strip, out, starts):
        def body(z, _):
            far = 125 - 8 * z
            for r in starts:
                rows, next_rows = slice(r, r + 8), slice(r + 1, r + 9)
                ex, ey, ez = (e_ref[i, z + shift, rows, :] for i in range(3))
                new = h_step(
                    ex, ey, ez, *(h_ref[h_base + i, z + 1, rows, :] for i in range(3)),
                    jnp.where(lane == 127, pltpu.roll(strip[0, rows, :], far, 1), pltpu.roll(ex, 127, 1)),
                    jnp.where(lane == 127, pltpu.roll(strip[2, rows, :], far, 1), pltpu.roll(ez, 127, 1)),
                    e_ref[1, z + shift, next_rows, :], e_ref[2, z + shift, next_rows, :],
                    e_ref[0, z + shift + 1, rows, :], e_ref[1, z + shift + 1, rows, :],
                )
                for i in range(3):
                    out[i, z + 1, rows, :] = new[i]
            return 0

        lax.fori_loop(0, NZ, body, 0, unroll=NZ)

    def main_curl(h_ref, z, r, strip):
        rows, back_rows = slice(r, r + 8), slice(r - 1, r + 7)
        far = 123 - 8 * z
        hx, hy, hz = (h_ref[i, z + 1, rows, :] for i in range(3))
        return curl(
            hx, hy, hz,
            jnp.where(lane == 0, pltpu.roll(strip[0, rows, :], far, 1), pltpu.roll(hx, 1, 1)),
            jnp.where(lane == 0, pltpu.roll(strip[2, rows, :], far, 1), pltpu.roll(hz, 1, 1)),
            h_ref[1, z + 1, back_rows, :], h_ref[2, z + 1, back_rows, :],
            h_ref[0, z, rows, :], h_ref[1, z, rows, :],
        )

    for c in (sends[4], sends[5], sends[8]):
        c.wait_recv()
    widen((0, 2), (8, 16))
    main_h(eh, 1, eh, 3, wide, h1, (8, 16))
    for c in sends[0:4] + sends[6:8] + sends[9:]:
        c.wait_recv()
    widen(range(6), (6, 14, 22))
    widen(range(8, 12), (7, 15, 23))
    strip_h(wide, wide, 3, sh1, (6, 14, 22))
    for r in (7, 15, 23):
        rows, back_rows = slice(r, r + 8), slice(r - 1, r + 7)
        hx, hy, hz = (sh1[i, rows, :] for i in range(3))
        turn = curl(
            hx, hy, hz, pltpu.roll(hx, 1, 1), pltpu.roll(hz, 1, 1),
            sh1[1, back_rows, :], sh1[2, back_rows, :], behind_z(hx), behind_z(hy),
        )
        d = wide[11, rows, :]
        for i in range(3):
            se1[i, rows, :] = wide[8 + i, rows, :] + d * turn[i]
    strip_h(se1, sh1, 0, sh2, (7, 15, 23))

    column = lax.broadcasted_iota(jnp.int32, (NZ, LANES), 1)
    start = 8 * lax.broadcasted_iota(jnp.int32, (NZ, LANES), 0)

    def pick(f, q):
        f = jnp.broadcast_to(f, (NZ, LANES))
        return jnp.sum(jnp.where(column == start + q, f, 0.0), axis=1, keepdims=True)

    def edge_lanes(f, i, row):
        line = se1[i, row : row + 1, :]
        return jnp.where(column == 127, pick(line, 1), jnp.where(column == 0, pick(line, 6), f))

    at, layers, shifted = slice(7, 8), slice(0, NZ), slice(1, NZ + 1)
    hy_row = income[0] + fix[0]
    hz_row = jnp.where(column == 127, pick(sh1[2, at, :], 1), income[1] + fix[1])
    d = income[5]
    e_row = [
        edge_lanes(f, i, 7)
        for i, f in enumerate((income[2] + d * fix[2], income[3] - d * fix[1], income[4] + d * fix[0]))
    ]
    h1[1, shifted, 7, :] = hy_row
    h1[2, shifted, 7, :] = hz_row
    for i in range(3):
        e1[i, layers, 7, :] = e_row[i]
    d = income[8]
    e1[1, layers, 24, :] = edge_lanes(income[6] + d * h1[2, shifted, 23, :], 1, 24)
    e1[2, layers, 24, :] = edge_lanes(income[7] - d * h1[1, shifted, 23, :], 2, 24)

    def first_e(z, _):
        for r in (8, 16):
            rows = slice(r, r + 8)
            turn = main_curl(h1, z, r, sh1)
            d = ad[3, z, rows, :]
            for i in range(3):
                e1[i, z, rows, :] = ad[i, z, rows, :] + d * turn[i]
        return 0

    lax.fori_loop(0, NZ, first_e, 0, unroll=NZ)
    main_h(e1, 0, h1, 0, se1, h2, (8, 16))
    ex, ey, ez = e_row
    ex_y = jnp.where(column == 127, pick(se1[0, at, :], 2), pltpu.roll(ex, 127, 1))
    h2[1, shifted, 7, :] = hy_row - DT * ((e1[0, shifted, 7, :] - ex) - (e1[2, layers, 8, :] - ez))
    h2[2, shifted, 7, :] = hz_row - DT * ((e1[1, layers, 8, :] - ey) - (ex_y - ex))

    def second_e(z, _):
        for b in (0, 8):
            rows, here = slice(TOP + b, TOP + b + 8), slice(b, b + 8)
            turn = main_curl(h2, z, TOP + b, sh2)
            d, factor = ad[3, z, rows, :], keep[z, here, :]
            for i in range(3):
                h_out[i, z, here, :] = h2[i, z + 1, rows, :]
                e_out[i, z, here, :] = factor * e1[i, z, rows, :] + d * turn[i] + late[i, z, here, :]
        return 0

    lax.fori_loop(0, NZ, second_e, 0, unroll=NZ)
    for c in sends:
        c.wait_send()


def write_out(e_ref, h_ref, e_out, h_out, sem):
    copies = [pltpu.make_async_copy(e_ref, e_out, sem.at[0]), pltpu.make_async_copy(h_ref, h_out, sem.at[1])]
    for c in copies:
        c.start()
    for c in copies:
        c.wait()


def body(e_field, h_field, pole_now, pole_prev, material, eps_inf, resonance, damping, strength):
    hbm = pl.BlockSpec(memory_space=pltpu.HBM)
    vmem = pl.BlockSpec(memory_space=pltpu.VMEM)
    f32 = jnp.float32
    block = pltpu.VMEM(e_field.shape, f32)
    operands = (
        e_field, h_field, pole_now, pole_prev, material,
        eps_inf, resonance.T, damping.T, strength.T,
    )
    operands = [pltpu.with_memory_space_constraint(x, pltpu.HBM) for x in operands]
    fields = pl.pallas_call(
        kernel,
        out_shape=(block, block),
        in_specs=[hbm] * 9,
        out_specs=(vmem, vmem),
        scratch_shapes=[
            pltpu.SMEM((4,), f32),
            pltpu.SMEM((2, 4), f32),
            pltpu.SMEM((2, 4), f32),
            pltpu.SMEM((2, 4), f32),
            pltpu.VMEM((6, NZ + 2, 40, LANES), f32),
            pltpu.VMEM((4, NZ, 40, LANES), f32),
            pltpu.VMEM(pole_now.shape, f32),
            pltpu.VMEM(pole_prev.shape, f32),
            pltpu.VMEM(material.shape, jnp.int32),
            pltpu.VMEM((11, 4) + TILE, f32),
            pltpu.VMEM((NZ, ROWS, LANES), f32),
            pltpu.VMEM((3, NZ, ROWS, LANES), f32),
            pltpu.VMEM((3, NZ + 1, 40, LANES), f32),
            pltpu.VMEM((3, NZ + 1, 40, LANES), f32),
            pltpu.VMEM((3, NZ + 1, 40, LANES), f32),
            pltpu.VMEM((4, 3, 40, LANES), f32),
            pltpu.VMEM((12, 40, LANES), f32),
            pltpu.VMEM((3, 40, LANES), f32),
            pltpu.VMEM((3, 40, LANES), f32),
            pltpu.VMEM((3, 40, LANES), f32),
            pltpu.VMEM((4, 3, 32, LANES), f32),
            pltpu.VMEM((3, 3, 32, LANES), f32),
            pltpu.VMEM((2, 3, 32, LANES), f32),
            pltpu.VMEM((9, NZ, LANES), f32),
            pltpu.VMEM((9, NZ, LANES), f32),
            pltpu.VMEM((3, NZ, LANES), f32),
            pltpu.SemaphoreType.DMA((16,)),
            pltpu.SemaphoreType.DMA((11,)),
            pltpu.SemaphoreType.DMA((11,)),
        ],
        compiler_params=pltpu.CompilerParams(
            collective_id=0, has_side_effects=True, vmem_limit_bytes=48 * 1024 * 1024
        ),
    )(*operands)
    fields = [pltpu.with_memory_space_constraint(x, pltpu.VMEM) for x in fields]
    return pl.pallas_call(
        write_out,
        out_shape=(pltpu.HBM(e_field.shape, f32),) * 2,
        in_specs=[vmem, vmem],
        out_specs=(hbm, hbm),
        scratch_shapes=[pltpu.SemaphoreType.DMA((2,))],
    )(*fields)


def solution(mesh):
    field = P(None, None, "gx", "gy")
    pole = P(None, None, None, "gx", "gy")
    in_specs = (field, field, pole, pole, P(None, "gx", "gy"), P(), P(), P(), P())
    return jax.shard_map(
        body, mesh=mesh, in_specs=in_specs, out_specs=(field, field), check_vma=False
    )
```
